32 devices in a mesh: gx: 8 (over z, x), gy: 4 (over y, core).
Axes of the slice: x: 2, y: 2, z: 4, core: 2. Of those that a mesh axis runs over, the one named last changes fastest.
Arguments:
- queries: bfloat16 [128, 128, 128], P('gx', 'gy'), may hold values from -6 to 6
- keys: bfloat16 [128, 128, 128], P('gx', 'gy'), may hold values from -6 to 6
- values: bfloat16 [128, 128, 128], P('gx', 'gy'), may hold values from -6 to 6
- out_attn: bfloat16 [128, 128, 128], P('gx', 'gy'), may hold values from -6 to 6
- out_grad: bfloat16 [128, 128, 128], P('gx', 'gy'), may hold values from -6 to 6
- log_norm: bfloat16 [4, 128, 128], P(None, 'gx', 'gy'), may hold values from 3 to 4
- neighbour_blocks: int32 [8, 16, 3], P('gx', 'gy'), may hold values from 0 to 15, as said below
- stencil: float32 [5, 128], replicated, may hold values from -3 to 3
Outputs:
- query_grad: bfloat16 [128, 128, 128], P('gx', 'gy')
- key_grad: bfloat16 [128, 128, 128], P('gx', 'gy')
- value_grad: bfloat16 [128, 128, 128], P('gx', 'gy')
- stencil_grad: float32 [5, 128], replicated
The draws below stay inside these ranges and needn't reach their ends.
Inputs may be any that keep to these rules, and one draw needn't show every extreme that they name: `neighbour_blocks`: among the entries of the 4 row blocks of one tile, at most 3 name blocks of any one tile of the strip (the tile of block c is c // 4), and exactly 3 do for some tile.
All inputs are finite; a program needn't handle non-finite values.
Results may differ from the reference program's by a relative error of at most 0.0054.
Values may be sent and summed in bfloat16 or wider, within the bound.
A program may use at most 64 MiB of HBM per device.

```python
import math
import jax
import jax.numpy as jnp
from jax import lax

PX = 16
PY = 32
BLOCK = 128
HEADS = 4
NB = 3
F = 128
RB = 4
GRID_X = 128
GRID_Y = 128
N_GX = 8
N_GY = 4


def draw_neighbour_blocks(key, part):
    row_blocks = PX * PY // BLOCK
    pair_count = row_blocks * NB
    capacity = max(2, (pair_count + N_GY - 1) // N_GY)
    first, second, third, fourth, fifth = jax.random.split(jax.random.fold_in(key, 11), 5)
    hot_base = jax.random.randint(first, (N_GX, 1), 0, N_GY)
    coin = jax.random.randint(second, (N_GX, N_GY), 0, 2)
    other = jax.random.randint(third, (N_GX, N_GY), 0, N_GY)
    hottest = jnp.where(coin == 0, hot_base, other)
    perm_keys = jax.random.split(fourth, N_GX * N_GY)
    orders = jax.vmap(lambda single: jax.random.permutation(single, pair_count))(perm_keys)
    orders = orders.reshape(N_GX, N_GY, pair_count).astype(jnp.int32)
    group = orders // capacity
    owner = (hottest[..., None] + group) % N_GY
    inner = jax.random.randint(fifth, (N_GX, N_GY, pair_count), 0, row_blocks)
    columns = owner * row_blocks + inner
    return columns.reshape(N_GX, N_GY * row_blocks, NB).astype(jnp.int32)


def block_levels(key, dims, shards, least, top_value):
    gain = 1.0
    for position, shards_of in shards:
        steps = jax.random.uniform(jax.random.fold_in(jax.random.fold_in(key, 6), position), (shards_of,), jnp.float32, least / len(shards), top_value / len(shards))
        gain = gain * jnp.repeat(jnp.exp(steps), dims[position] // shards_of).reshape((-1,) + (1,) * (len(dims) - 1 - position))
    return gain


def bell_draw(own_key, extent, scale, reach, shards=(), kind=jnp.bfloat16):
    level = block_levels(own_key, extent, shards, -0.22, 0.18) if shards else 1.0
    entries = jax.random.normal(own_key, extent, jnp.float32) * scale * level
    return jnp.minimum(jnp.maximum(entries, -reach), reach).astype(kind)


def setup_inputs(seed: int = 0) -> dict:
    streams_of = jax.random.split(jax.random.key(seed), 9)
    return {
        "queries": bell_draw(streams_of[0], (GRID_X, GRID_Y, F), 1.0, 6.0, ((0, 8), (1, 4))),
        "keys": bell_draw(streams_of[1], (GRID_X, GRID_Y, F), 1.0, 6.0, ((0, 8), (1, 4))),
        "values": bell_draw(streams_of[2], (GRID_X, GRID_Y, F), 1.0, 6.0, ((0, 8), (1, 4))),
        "out_attn": bell_draw(streams_of[3], (GRID_X, GRID_Y, F), 1.0, 6.0, ((0, 8), (1, 4))),
        "out_grad": bell_draw(streams_of[4], (GRID_X, GRID_Y, F), 1.0, 6.0, ((0, 8), (1, 4))),
        "log_norm": jnp.clip(3.0 + 1.0 * jax.random.uniform(streams_of[5], (HEADS, GRID_X, GRID_Y), jnp.float32) ** block_levels(streams_of[5], (HEADS, GRID_X, GRID_Y), ((1, 8), (2, 4)), -0.2, 0.2), 3.0, 4.0).astype(jnp.bfloat16),
        "neighbour_blocks": draw_neighbour_blocks(jax.random.fold_in(streams_of[8], 71), 0),
        "stencil": bell_draw(streams_of[7], (5, F), 0.5, 3.0, (), jnp.float32),
    }


def tile_grads(query_rows, grad_rows, stat_rows, key_rows, value_rows, head_count):
    item_count = query_rows.shape[0]
    block_rows = query_rows.shape[1]
    features = query_rows.shape[2]
    head_width = features // head_count
    softmax_scale = 1.0 / math.sqrt(head_width)
    shape_four = (item_count, block_rows, head_count, head_width)
    query_heads = query_rows.reshape(shape_four).astype(jnp.float32)
    grad_heads = grad_rows.reshape(shape_four).astype(jnp.float32)
    key_heads = key_rows.reshape(shape_four).astype(jnp.float32)
    value_heads = value_rows.reshape(shape_four).astype(jnp.float32)
    log_part = stat_rows[:, 0].astype(jnp.float32)
    delta_part = stat_rows[:, 1].astype(jnp.float32)
    scores = jnp.einsum('sqhd,skhd->shqk', query_heads, key_heads) * softmax_scale
    weights = jnp.exp(scores - log_part[..., None])
    weight_grad = jnp.einsum('sqhd,skhd->shqk', grad_heads, value_heads)
    score_grad = weights * (weight_grad - delta_part[..., None])
    weights_low = lax.optimization_barrier(weights.astype(jnp.bfloat16)).astype(jnp.float32)
    score_low = lax.optimization_barrier(score_grad.astype(jnp.bfloat16)).astype(jnp.float32)
    value_part = jnp.einsum('shqk,sqhd->skhd', weights_low, grad_heads)
    key_part = jnp.einsum('shqk,sqhd->skhd', score_low, query_heads) * softmax_scale
    query_part = jnp.einsum('shqk,skhd->sqhd', score_low, key_heads) * softmax_scale
    flat_shape = (item_count, block_rows, features)
    return (query_part.reshape(flat_shape), key_part.reshape(flat_shape), value_part.reshape(flat_shape))

def to_blocks(array):
    features = array.shape[-1]
    shaped = array.reshape(N_GX, PX, N_GY, PY, features).transpose(0, 2, 1, 3, 4)
    return shaped.reshape(N_GX, N_GY * RB, BLOCK, features)

def from_blocks(blocks):
    features = blocks.shape[-1]
    shaped = blocks.reshape(N_GX, N_GY, PX, PY, features).transpose(0, 2, 1, 3, 4)
    return shaped.reshape(GRID_X, GRID_Y, features)

def reference(queries, keys, values, out_attn, out_grad, log_norm, neighbour_blocks, stencil):
    features = queries.shape[-1]
    head_width = features // HEADS
    products = out_grad.astype(jnp.float32) * out_attn.astype(jnp.float32)
    delta = products.reshape(GRID_X, GRID_Y, HEADS, head_width).sum(-1).astype(jnp.bfloat16)
    stat_grid = jnp.stack([log_norm, delta.transpose(2, 0, 1)], 0)
    stat_blocks = stat_grid.reshape(2, HEADS, N_GX, PX, N_GY, PY).transpose(2, 4, 0, 1, 3, 5)
    stat_blocks = stat_blocks.reshape(N_GX, N_GY, 2, HEADS, RB, BLOCK).transpose(0, 1, 4, 2, 3, 5)
    stat_blocks = stat_blocks.reshape(N_GX, N_GY * RB, 2, HEADS, BLOCK)
    strip_count = N_GY * RB
    width = NB + 1

    def strip_grads(strip):
        query_strip, key_strip, value_strip, grad_strip, stat_strip, list_strip = strip
        own = jnp.arange(strip_count, dtype=jnp.int32)[:, None]
        chosen = jnp.concatenate([own, list_strip.astype(jnp.int32)], 1)
        flat = chosen.reshape(-1)
        query_part, key_part, value_part = tile_grads(jnp.repeat(query_strip, width, axis=0), jnp.repeat(grad_strip, width, axis=0), jnp.repeat(stat_strip, width, axis=0), key_strip[flat], value_strip[flat], HEADS)
        query_sum = query_part.reshape(strip_count, width, BLOCK, features).sum(1)
        key_sum = jax.ops.segment_sum(key_part, flat, num_segments=strip_count)
        value_sum = jax.ops.segment_sum(value_part, flat, num_segments=strip_count)
        return (query_sum, key_sum, value_sum)
    query_all, key_all, value_all = lax.map(strip_grads, (to_blocks(queries), to_blocks(keys), to_blocks(values), to_blocks(out_grad), stat_blocks, neighbour_blocks))
    grad_float = out_grad.astype(jnp.float32)
    value_float = values.astype(jnp.float32)
    moved = [grad_float, jnp.roll(grad_float, -1, 0), jnp.roll(grad_float, 1, 0), jnp.roll(grad_float, -1, 1), jnp.roll(grad_float, 1, 1)]
    stencil_term = stencil[0] * moved[0]
    for index in range(1, 5):
        stencil_term = stencil_term + stencil[index] * moved[index]
    rows_list = [lax.optimization_barrier(jnp.sum(moved[index] * value_float, axis=(0, 1))) for index in range(5)]
    stencil_grad = jnp.stack(rows_list) / math.sqrt(GRID_X * GRID_Y)
    query_grad = from_blocks(query_all).astype(jnp.bfloat16)
    key_grad = from_blocks(key_all).astype(jnp.bfloat16)
    value_grad = (from_blocks(value_all) + stencil_term).astype(jnp.bfloat16)
    return (query_grad, key_grad, value_grad, stencil_grad)
```

```python
import functools
import math

import jax
import jax.numpy as jnp
from jax import lax
from jax.experimental import pallas as pl
from jax.experimental.pallas import tpu as pltpu
from jax.sharding import PartitionSpec as P

BLOCK = 128
HEADS = 4
LOG2E = 1.4426950408889634
F32 = jnp.float32
BF16 = jnp.bfloat16


def dot(a, b):
    return jnp.dot(a, b, preferred_element_type=F32)


def dot_nt(a, b):
    return lax.dot_general(a, b, (((1,), (1,)), ((), ())), preferred_element_type=F32)


def iota(shape, dim):
    return lax.broadcasted_iota(jnp.int32, shape, dim)


def kernel(
    nx, n, tx, ty, rb, listed, cap,
    q_ref, k_ref, v_ref, o_ref, g_ref, ln_ref, nb_ref, w_ref,
    dq_ref, dk_ref, dv_ref, sg_ref,
    q_in, g_in, st_own, st_all, nb_all, nb_own, nb_s, kmt, edge, xh, yh,
    dq_acc, dk_acc, dv_acc, dk_part, dv_part, ret_out, ret_in,
    part, col_all, row_sum, row_all,
    big_send, big_recv, small_send, small_recv, halo_send, halo_recv,
    ret_send, ret_recv, col_send, col_recv, row_send, row_recv, local_sem,
):
    f = q_ref.shape[2]
    pts = rb * BLOCK
    hw = f // HEADS
    scale = 1.0 / math.sqrt(hw)
    mx = lax.axis_index("gx")
    my = lax.axis_index("gy")
    half = n // 2
    sib = my + 1 - 2 * lax.rem(my, 2)

    def peer(t):
        return lax.rem(my + t, n)

    def xpeer(t):
        return lax.rem(mx + t, nx)

    barrier = pltpu.get_barrier_semaphore()
    for t in range(1, n):
        pl.semaphore_signal(barrier, inc=1, device_id=(mx, peer(t)), device_id_type=pl.DeviceIdType.MESH)

    def greet(t, carry):
        pl.semaphore_signal(barrier, inc=1, device_id=(xpeer(t), my), device_id_type=pl.DeviceIdType.MESH)
        return carry

    lax.fori_loop(1, nx, greet, 0)

    def remote(src, dst, ssem, rsem, x, y):
        return pltpu.make_async_remote_copy(
            src_ref=src, dst_ref=dst, send_sem=ssem, recv_sem=rsem,
            device_id=(x, y), device_id_type=pl.DeviceIdType.MESH,
        )

    nb_own[...] = jnp.zeros_like(nb_own)
    nb_own[0:rb, 0:listed] = nb_ref[0]
    g2 = g_ref[...].reshape(pts, f)
    rows_of = iota((2 * tx, pts), 0)
    want = jnp.where(rows_of < tx, rows_of * ty, (rows_of - tx) * ty + ty - 1)
    pick = (iota((2 * tx, pts), 1) == want).astype(F32).astype(BF16)
    edge[...] = dot(pick, g2).astype(BF16).reshape(2, tx, f)

    prod = g2.astype(F32) * o_ref[...].reshape(pts, f).astype(F32)
    high = prod.astype(BF16)
    low = (prod - high.astype(F32)).astype(BF16)
    head_row = iota((2 * HEADS, f), 0) - HEADS
    summing = (iota((2 * HEADS, f), 1) // hw == head_row).astype(F32).astype(BF16)
    lines = BLOCK // ty
    ln = ln_ref[...].astype(F32).reshape(HEADS * tx, ty)
    ln = jnp.concatenate([ln] * lines, axis=1)
    ln = jnp.where(
        iota(ln.shape, 1) // ty == lax.rem(iota(ln.shape, 0), lines), ln, 0.0
    ).astype(BF16)
    gr = iota((rb * 2 * HEADS, HEADS * tx), 0)
    gc = iota((rb * 2 * HEADS, HEADS * tx), 1)
    gather = (
        (gc // tx == lax.rem(gr, 2 * HEADS)) & (lax.rem(gc, tx) // lines == gr // (2 * HEADS))
    ).astype(F32).astype(BF16)
    ln_rows = dot(gather, ln) * LOG2E
    for b in range(rb):
        sl = slice(b * BLOCK, (b + 1) * BLOCK)
        delta = dot_nt(summing, high[sl]) + dot_nt(summing, low[sl])
        delta = delta.astype(BF16).astype(F32)
        st_own[b] = ln_rows[b * 2 * HEADS:(b + 1) * 2 * HEADS] + delta

    pl.semaphore_wait(barrier, n - 1 + nx - 1)

    big = []
    targets = [(0, sib)] + [(t, peer(2 * t)) for t in range(1, half)]
    for t, to in targets[1:] + targets[:1]:
        at = 1 + t
        big.append(remote(q_ref, q_in[t], big_send.at[at, 0], big_recv.at[at, 0], mx, to))
        big.append(remote(g_ref, g_in[t], big_send.at[at, 1], big_recv.at[at, 1], mx, to))
    halo = [
        remote(edge.at[0], yh.at[0], halo_send.at[0], halo_recv.at[0], mx, peer(n - 1)),
        remote(edge.at[1], yh.at[1], halo_send.at[1], halo_recv.at[1], mx, peer(1)),
        remote(g_ref.at[0, pl.ds(0, ty)], xh.at[0], halo_send.at[2], halo_recv.at[2], xpeer(nx - 1), my),
        remote(g_ref.at[rb - 1, pl.ds(BLOCK - ty, ty)], xh.at[1], halo_send.at[3], halo_recv.at[3], xpeer(1), my),
    ]
    small = []
    for t in range(1, n):
        small.append(remote(nb_own, nb_all.at[my], small_send.at[t, 0], small_recv.at[t, 0], mx, peer(t)))
        small.append(remote(st_own, st_all.at[my], small_send.at[t, 1], small_recv.at[t, 1], mx, peer(t)))
    for copy in halo + small + big:
        copy.start()

    def wait_big(number, which):
        ref = (q_in, g_in)[which][number - 1]
        remote(
            ref, ref, big_send.at[number, which], big_recv.at[number, which], mx, sib
        ).wait_recv()

    lane_head = iota((BLOCK, f), 1) // hw
    row_head = iota((f, BLOCK), 0) // hw

    def by_head(x):
        return [jnp.where(lane_head == h, x, jnp.zeros_like(x)) for h in range(HEADS)]

    def item(q, g, st, k, v, kt):
        qs, gs = by_head(q), by_head(g)
        probs, grads = [], []
        for h in range(HEADS):
            s = dot_nt(k, qs[h])
            dp = dot_nt(v, gs[h])
            p = jnp.exp2(s * (scale * LOG2E) - st[h:h + 1])
            d = p * (dp - st[HEADS + h:HEADS + h + 1])
            probs.append(p.astype(BF16))
            grads.append(d.astype(BF16))
        dv = dot(jnp.concatenate(probs, 1), jnp.concatenate(gs, 0))
        dk = dot(jnp.concatenate(grads, 1), jnp.concatenate(qs, 0)) * scale
        dqt = dot(kt, jnp.concatenate(grads, 0)) * scale
        return dqt, dk, dv

    for b in range(rb):
        k = k_ref[b]
        ktr = k.astype(F32).T.astype(BF16)
        kt = jnp.concatenate(
            [jnp.where(row_head == h, ktr, jnp.zeros_like(ktr)) for h in range(HEADS)], 1
        )
        kmt[b] = kt
        dqt, dk, dv = item(q_ref[b], g_ref[b], st_own[b], k, v_ref[b], kt)
        dq_acc[b] = dqt
        dk_acc[b] = dk
        dv_acc[b] = dv

    for copy in halo:
        copy.wait_recv()
    g32 = g2.astype(F32)
    v32 = v_ref[...].reshape(pts, f).astype(F32)
    pr = iota((pts, tx), 0)
    pc = iota((pts, tx), 1)
    put_next = (pr == pc * ty + ty - 1).astype(F32).astype(BF16)
    put_prev = (pr == pc * ty).astype(F32).astype(BF16)
    ycol = lax.rem(iota((pts, f), 0), ty)
    y_next = jnp.where(ycol == ty - 1, dot(put_next, yh[0]), pltpu.roll(g32, pts - 1, 0))
    y_prev = jnp.where(ycol == 0, dot(put_prev, yh[1]), pltpu.roll(g32, 1, 0))
    x_next = jnp.concatenate([g32[ty:], xh[0].astype(F32)], 0)
    x_prev = jnp.concatenate([xh[1].astype(F32), g32[:-ty]], 0)
    part[...] = jnp.zeros_like(part)
    term = None
    for index, moved in enumerate([g32, x_next, x_prev, y_next, y_prev]):
        part[index:index + 1] = jnp.sum(moved * v32, axis=0, keepdims=True)
        scaled = w_ref[index:index + 1] * moved
        term = scaled if term is None else term + scaled
    for b in range(rb):
        dv_acc[b] += term[b * BLOCK:(b + 1) * BLOCK]

    cols = [
        remote(part, col_all.at[my], col_send.at[t], col_recv.at[t], mx, peer(t)) for t in range(1, n)
    ]
    for copy in cols:
        copy.start()
    col_all[my] = part[...]

    for t in range(1, n):
        small[2 * (t - 1)].wait_recv()
    nb_all[my] = nb_own[...]
    to_smem = pltpu.make_async_copy(nb_all, nb_s, local_sem)
    to_smem.start()
    to_smem.wait()

    def slots(src):
        rows = [jnp.int32(0)] * cap
        inner = [jnp.int32(0)] * cap
        count = jnp.int32(0)
        for r in range(rb):
            for j in range(listed):
                value = nb_s[src, r, j]
                mine = lax.div(value, rb) == my
                for c in range(cap):
                    here = mine & (count == c)
                    rows[c] = jnp.where(here, r, rows[c])
                    inner[c] = jnp.where(here, lax.rem(value, rb), inner[c])
                count = count + mine.astype(jnp.int32)
        return rows, inner, count

    forwards = []

    def pass_on(which):
        for t in range(1, half):
            wait_big(1 + t, which)
            ref = (q_in, g_in)[which]
            copy = remote(
                ref[t], ref[half + t - 1],
                big_send.at[half + t, which], big_recv.at[half + t, which], mx, sib,
            )
            copy.start()
            forwards.append(copy)

    keyed = []
    returns = []

    def work(src, number):
        rows, inner, count = slots(src)
        own = number == 0
        q_from = q_ref if own else q_in[number - 1]
        g_from = g_ref if own else g_in[number - 1]
        for c in range(cap):
            at = number * cap + c
            r, i = rows[c], inner[c]
            q, g = q_from[r], g_from[r]
            st = st_own[r] if own else st_all[src, r]
            dqt, dk, dv = item(q, g, st, k_ref[i], v_ref[i], kmt[i])
            dk_part[at] = dk
            dv_part[at] = dv
            keyed.append(jnp.where(count > c, i, -1))
            if own:
                ret_in[my * cap + c] = dqt.astype(BF16)
            else:
                ret_out[at] = dqt.astype(BF16)
                copy = remote(
                    ret_out.at[at], ret_in.at[my * cap + c],
                    ret_send.at[at], ret_recv.at[at], mx, src,
                )
                copy.start()
                returns.append(copy)

    work(my, 0)
    pass_on(0)
    wait_big(1, 0)
    wait_big(1, 1)
    for t in range(1, n):
        small[2 * (t - 1) + 1].wait_recv()
    work(sib, 1)
    pass_on(1)

    for copy in cols:
        copy.wait_recv()
    total = col_all[0]
    for d in range(1, n):
        total = total + col_all[d]
    row_sum[...] = total
    row_all[mx] = total

    def row_copy(t):
        return remote(row_sum, row_all.at[mx], row_send.at[t], row_recv.at[t], xpeer(t), my)

    def send_row(t, carry):
        row_copy(t).start()
        return carry

    lax.fori_loop(1, nx, send_row, 0)

    for t in range(1, half):
        work(lax.rem(my + n - 2 * t, n), 1 + t)
    for t in range(1, half):
        wait_big(half + t, 0)
        wait_big(half + t, 1)
        work(lax.rem(sib + n - 2 * t, n), half + t)

    for b in range(rb):
        dk = dk_acc[b]
        dv = dv_acc[b]
        for at in range(n * cap):
            hit = jnp.full((BLOCK, f), keyed[at], jnp.int32) == b
            dk = dk + jnp.where(hit, dk_part[at], 0.0)
            dv = dv + jnp.where(hit, dv_part[at], 0.0)
        dk_ref[b * BLOCK:(b + 1) * BLOCK] = dk.astype(BF16)
        dv_ref[b * BLOCK:(b + 1) * BLOCK] = dv.astype(BF16)

    def get_row(t, carry):
        row_copy(t).wait_recv()
        return carry

    lax.fori_loop(1, nx, get_row, 0)
    total = lax.fori_loop(1, nx, lambda d, acc: acc + row_all[d], row_all[0])
    sg_ref[...] = total / math.sqrt(pts * nx * n)

    for copy in returns:
        copy.wait_recv()
    place = []
    for r in range(rb):
        for j in range(listed):
            value = nb_s[my, r, j]
            place.append(lax.div(value, rb))
    for r in range(rb):
        dqt = dq_acc[r]
        for j in range(listed):
            e = r * listed + j
            rank = jnp.int32(0)
            for before in range(e):
                rank = rank + (place[before] == place[e]).astype(jnp.int32)
            dqt = dqt + ret_in[place[e] * cap + rank].astype(F32)
        dq_ref[r * BLOCK:(r + 1) * BLOCK] = dqt.T.astype(BF16)

    for copy in halo + small + big + cols + forwards + returns:
        copy.wait_send()

    def end_row(t, carry):
        row_copy(t).wait_send()
        return carry

    lax.fori_loop(1, nx, end_row, 0)


def per_device(nx, n, queries, keys, values, out_attn, out_grad, log_norm, neighbour_blocks, stencil):
    tx, ty, f = queries.shape
    pts = tx * ty
    rb = pts // BLOCK
    listed = neighbour_blocks.shape[2]
    cap = max(2, (rb * listed + n - 1) // n)
    flat = [a.reshape(rb, BLOCK, f) for a in (queries, keys, values, out_attn, out_grad)]
    vmem = pl.BlockSpec(memory_space=pltpu.VMEM)
    half = n // 2
    dma = pltpu.SemaphoreType.DMA
    grads = jax.ShapeDtypeStruct((pts, f), BF16)
    dq, dk, dv, sg = pl.pallas_call(
        functools.partial(kernel, nx, n, tx, ty, rb, listed, cap),
        out_shape=[grads, grads, grads, jax.ShapeDtypeStruct((8, f), F32)],
        in_specs=[vmem] * 8,
        out_specs=[vmem] * 4,
        scratch_shapes=[
            [pltpu.VMEM((rb, BLOCK, f), BF16)] * (n - 1),
            [pltpu.VMEM((rb, BLOCK, f), BF16)] * (n - 1),
            pltpu.VMEM((rb, 2 * HEADS, BLOCK), F32),
            pltpu.VMEM((n, rb, 2 * HEADS, BLOCK), F32),
            pltpu.VMEM((n, 8, 128), jnp.int32),
            pltpu.VMEM((8, 128), jnp.int32),
            pltpu.SMEM((n, 8, 128), jnp.int32),
            pltpu.VMEM((rb, f, HEADS * BLOCK), BF16),
            pltpu.VMEM((2, tx, f), BF16),
            pltpu.VMEM((2, ty, f), BF16),
            pltpu.VMEM((2, tx, f), BF16),
            pltpu.VMEM((rb, f, BLOCK), F32),
            pltpu.VMEM((rb, BLOCK, f), F32),
            pltpu.VMEM((rb, BLOCK, f), F32),
            pltpu.VMEM((n * cap, BLOCK, f), F32),
            pltpu.VMEM((n * cap, BLOCK, f), F32),
            pltpu.VMEM((n * cap, f, BLOCK), BF16),
            pltpu.VMEM((n * cap, f, BLOCK), BF16),
            pltpu.VMEM((8, f), F32),
            pltpu.VMEM((n, 8, f), F32),
            pltpu.VMEM((8, f), F32),
            pltpu.VMEM((nx, 8, f), F32),
            dma((n, 2)), dma((n, 2)),
            dma((n, 2)), dma((n, 2)),
            dma((4,)), dma((4,)),
            dma((n * cap,)), dma((n * cap,)),
            dma((n,)), dma((n,)),
            dma((nx,)), dma((nx,)),
            dma,
        ],
        compiler_params=pltpu.CompilerParams(
            collective_id=0, has_side_effects=True, vmem_limit_bytes=40 * 1024 * 1024
        ),
    )(*flat, log_norm, neighbour_blocks, stencil)
    shape = (tx, ty, f)
    return dq.reshape(shape), dk.reshape(shape), dv.reshape(shape), sg[:5]


def solution(mesh):
    placed = (
        P("gx", "gy", None),
        P("gx", "gy", None),
        P("gx", "gy", None),
        P("gx", "gy", None),
        P("gx", "gy", None),
        P(None, "gx", "gy"),
        P("gx", "gy", None),
        P(),
    )
    return jax.shard_map(
        functools.partial(per_device, mesh.shape["gx"], mesh.shape["gy"]),
        mesh=mesh,
        in_specs=placed,
        out_specs=(P("gx", "gy", None), P("gx", "gy", None), P("gx", "gy", None), P()),
        check_vma=False,
    )
```

```python
import functools
import math

import jax
import jax.numpy as jnp
from jax import lax
from jax.experimental import pallas as pl
from jax.experimental.pallas import tpu as pltpu
from jax.sharding import PartitionSpec as P

BLOCK = 128
HEADS = 4
LOG2E = 1.4426950408889634
F32 = jnp.float32
BF16 = jnp.bfloat16


def dot(a, b):
    return jnp.dot(a, b, preferred_element_type=F32)


def dot_nt(a, b):
    return lax.dot_general(a, b, (((1,), (1,)), ((), ())), preferred_element_type=F32)


def iota(shape, dim):
    return lax.broadcasted_iota(jnp.int32, shape, dim)


def kernel(
    nx, n, tx, ty, rb, listed, cap,
    q_hbm, k_hbm, v_hbm, o_hbm, g_hbm, ln_hbm, w_hbm, nb_ref,
    dq_hbm, dk_hbm, dv_hbm, sg_hbm,
    dq_ref, dk_ref, dv_ref, sg_ref, store_sem,
    q_ref, k_ref, v_ref, o_ref, g_ref, ln_ref, w_ref, load_sem,
    q_in, g_in, st_own, st_all, nb_all, nb_own, nb_s, kmt, edge, xh, yh,
    dq_acc, dk_acc, dv_acc, dk_part, dv_part, ret_out, ret_in,
    part, col_all, row_sum, row_all,
    big_send, big_recv, small_send, small_recv, halo_send, halo_recv,
    ret_send, ret_recv, col_send, col_recv, row_send, row_recv, local_sem,
):
    g_load, o_load, ln_load, k_load, v_load, q_load, w_load = [
        pltpu.make_async_copy(src, dst, load_sem.at[at])
        for at, (src, dst) in enumerate([
            (g_hbm, g_ref), (o_hbm, o_ref), (ln_hbm, ln_ref), (k_hbm, k_ref),
            (v_hbm, v_ref), (q_hbm, q_ref), (w_hbm, w_ref),
        ])
    ]
    f = q_ref.shape[2]
    pts = rb * BLOCK
    hw = f // HEADS
    scale = 1.0 / math.sqrt(hw)
    mx = lax.axis_index("gx")
    my = lax.axis_index("gy")
    half = n // 2
    sib = my + 1 - 2 * lax.rem(my, 2)

    def peer(t):
        return lax.rem(my + t, n)

    def xpeer(t):
        return lax.rem(mx + t, nx)

    barrier = pltpu.get_barrier_semaphore()
    for t in range(1, n):
        pl.semaphore_signal(barrier, inc=1, device_id=(mx, peer(t)), device_id_type=pl.DeviceIdType.MESH)

    def greet(t, carry):
        pl.semaphore_signal(barrier, inc=1, device_id=(xpeer(t), my), device_id_type=pl.DeviceIdType.MESH)
        return carry

    lax.fori_loop(1, nx, greet, 0)

    def remote(src, dst, ssem, rsem, x, y):
        return pltpu.make_async_remote_copy(
            src_ref=src, dst_ref=dst, send_sem=ssem, recv_sem=rsem,
            device_id=(x, y), device_id_type=pl.DeviceIdType.MESH,
        )

    for copy in (g_load, o_load, ln_load, k_load, v_load, q_load, w_load):
        copy.start()
    nb_own[...] = jnp.zeros_like(nb_own)
    nb_own[0:rb, 0:listed] = nb_ref[0]
    pl.semaphore_wait(barrier, n - 1 + nx - 1)

    lists = [
        remote(nb_own, nb_all.at[my], small_send.at[t, 0], small_recv.at[t, 0], mx, peer(t))
        for t in range(1, n)
    ]
    big = []

    def send_big(t, which):
        to = sib if t == 0 else peer(2 * t)
        src, dst = ((q_hbm, q_in), (g_hbm, g_in))[which]
        big.append(remote(
            src, dst[t], big_send.at[1 + t, which], big_recv.at[1 + t, which], mx, to
        ))
        big[-1].start()

    for copy in lists:
        copy.start()
    for t in range(1, half):
        send_big(t, 0)

    g_load.wait()
    o_load.wait()
    ln_load.wait()
    g2 = g_ref[...].reshape(pts, f)
    rows_of = iota((2 * tx, pts), 0)
    want = jnp.where(rows_of < tx, rows_of * ty, (rows_of - tx) * ty + ty - 1)
    pick = (iota((2 * tx, pts), 1) == want).astype(F32).astype(BF16)
    edge[...] = dot(pick, g2).astype(BF16).reshape(2, tx, f)

    prod = g2.astype(F32) * o_ref[...].reshape(pts, f).astype(F32)
    high = prod.astype(BF16)
    low = (prod - high.astype(F32)).astype(BF16)
    head_row = iota((2 * HEADS, f), 0) - HEADS
    summing = (iota((2 * HEADS, f), 1) // hw == head_row).astype(F32).astype(BF16)
    lines = BLOCK // ty
    ln = ln_ref[...].astype(F32).reshape(HEADS * tx, ty)
    ln = jnp.concatenate([ln] * lines, axis=1)
    ln = jnp.where(
        iota(ln.shape, 1) // ty == lax.rem(iota(ln.shape, 0), lines), ln, 0.0
    ).astype(BF16)
    gr = iota((rb * 2 * HEADS, HEADS * tx), 0)
    gc = iota((rb * 2 * HEADS, HEADS * tx), 1)
    gather = (
        (gc // tx == lax.rem(gr, 2 * HEADS)) & (lax.rem(gc, tx) // lines == gr // (2 * HEADS))
    ).astype(F32).astype(BF16)
    ln_rows = dot(gather, ln) * LOG2E
    for b in range(rb):
        sl = slice(b * BLOCK, (b + 1) * BLOCK)
        delta = dot_nt(summing, high[sl]) + dot_nt(summing, low[sl])
        delta = delta.astype(BF16).astype(F32)
        st_own[b] = ln_rows[b * 2 * HEADS:(b + 1) * 2 * HEADS] + delta

    halo = [
        remote(edge.at[0], yh.at[0], halo_send.at[0], halo_recv.at[0], mx, peer(n - 1)),
        remote(edge.at[1], yh.at[1], halo_send.at[1], halo_recv.at[1], mx, peer(1)),
        remote(g_ref.at[0, pl.ds(0, ty)], xh.at[0], halo_send.at[2], halo_recv.at[2], xpeer(nx - 1), my),
        remote(g_ref.at[rb - 1, pl.ds(BLOCK - ty, ty)], xh.at[1], halo_send.at[3], halo_recv.at[3], xpeer(1), my),
    ]
    stats = [
        remote(st_own, st_all.at[my], small_send.at[t, 1], small_recv.at[t, 1], mx, peer(t))
        for t in range(1, n)
    ]
    for copy in halo + stats:
        copy.start()
    for t in range(1, half):
        send_big(t, 1)
    send_big(0, 0)
    send_big(0, 1)

    def wait_big(number, which):
        ref = (q_in, g_in)[which][number - 1]
        remote(
            ref, ref, big_send.at[number, which], big_recv.at[number, which], mx, sib
        ).wait_recv()

    lane_head = iota((BLOCK, f), 1) // hw
    row_head = iota((f, BLOCK), 0) // hw

    def by_head(x):
        return [jnp.where(lane_head == h, x, jnp.zeros_like(x)) for h in range(HEADS)]

    def item(q, g, st, k, v, kt):
        qs, gs = by_head(q), by_head(g)
        probs, grads = [], []
        for h in range(HEADS):
            s = dot_nt(k, qs[h])
            dp = dot_nt(v, gs[h])
            p = jnp.exp2(s * (scale * LOG2E) - st[h:h + 1])
            d = p * (dp - st[HEADS + h:HEADS + h + 1])
            probs.append(p.astype(BF16))
            grads.append(d.astype(BF16))
        dv = dot(jnp.concatenate(probs, 1), jnp.concatenate(gs, 0))
        dk = dot(jnp.concatenate(grads, 1), jnp.concatenate(qs, 0)) * scale
        dqt = dot(kt, jnp.concatenate(grads, 0)) * scale
        return dqt, dk, dv

    for copy in (k_load, v_load, q_load, w_load):
        copy.wait()
    for b in range(rb):
        k = k_ref[b]
        ktr = k.astype(F32).T.astype(BF16)
        kt = jnp.concatenate(
            [jnp.where(row_head == h, ktr, jnp.zeros_like(ktr)) for h in range(HEADS)], 1
        )
        kmt[b] = kt
        dqt, dk, dv = item(q_ref[b], g_ref[b], st_own[b], k, v_ref[b], kt)
        dq_acc[b] = dqt
        dk_acc[b] = dk
        dv_acc[b] = dv

    for copy in halo:
        copy.wait_recv()
    g32 = g2.astype(F32)
    v32 = v_ref[...].reshape(pts, f).astype(F32)
    pr = iota((pts, tx), 0)
    pc = iota((pts, tx), 1)
    put_next = (pr == pc * ty + ty - 1).astype(F32).astype(BF16)
    put_prev = (pr == pc * ty).astype(F32).astype(BF16)
    ycol = lax.rem(iota((pts, f), 0), ty)
    y_next = jnp.where(ycol == ty - 1, dot(put_next, yh[0]), pltpu.roll(g32, pts - 1, 0))
    y_prev = jnp.where(ycol == 0, dot(put_prev, yh[1]), pltpu.roll(g32, 1, 0))
    x_next = jnp.concatenate([g32[ty:], xh[0].astype(F32)], 0)
    x_prev = jnp.concatenate([xh[1].astype(F32), g32[:-ty]], 0)
    part[...] = jnp.zeros_like(part)
    term = None
    for index, moved in enumerate([g32, x_next, x_prev, y_next, y_prev]):
        part[index:index + 1] = jnp.sum(moved * v32, axis=0, keepdims=True)
        scaled = w_ref[index:index + 1] * moved
        term = scaled if term is None else term + scaled
    for b in range(rb):
        dv_acc[b] += term[b * BLOCK:(b + 1) * BLOCK]

    cols = [
        remote(part, col_all.at[my], col_send.at[t], col_recv.at[t], mx, peer(t)) for t in range(1, n)
    ]
    for copy in cols:
        copy.start()
    col_all[my] = part[...]

    for copy in lists:
        copy.wait_recv()
    nb_all[my] = nb_own[...]
    to_smem = pltpu.make_async_copy(nb_all, nb_s, local_sem)
    to_smem.start()
    to_smem.wait()

    def slots(src):
        rows = [jnp.int32(0)] * cap
        inner = [jnp.int32(0)] * cap
        count = jnp.int32(0)
        for r in range(rb):
            for j in range(listed):
                value = nb_s[src, r, j]
                mine = lax.div(value, rb) == my
                for c in range(cap):
                    here = mine & (count == c)
                    rows[c] = jnp.where(here, r, rows[c])
                    inner[c] = jnp.where(here, lax.rem(value, rb), inner[c])
                count = count + mine.astype(jnp.int32)
        return rows, inner, count

    forwards = []

    def pass_on(which):
        for t in range(1, half):
            wait_big(1 + t, which)
            ref = (q_in, g_in)[which]
            copy = remote(
                ref[t], ref[half + t - 1],
                big_send.at[half + t, which], big_recv.at[half + t, which], mx, sib,
            )
            copy.start()
            forwards.append(copy)

    keyed = []
    returns = []

    def work(src, number):
        rows, inner, count = slots(src)
        own = number == 0
        q_from = q_ref if own else q_in[number - 1]
        g_from = g_ref if own else g_in[number - 1]
        for c in range(cap):
            at = number * cap + c
            r, i = rows[c], inner[c]
            q, g = q_from[r], g_from[r]
            st = st_own[r] if own else st_all[src, r]
            dqt, dk, dv = item(q, g, st, k_ref[i], v_ref[i], kmt[i])
            dk_part[at] = dk
            dv_part[at] = dv
            keyed.append(jnp.where(count > c, i, -1))
            if own:
                ret_in[my * cap + c] = dqt.astype(BF16)
            else:
                ret_out[at] = dqt.astype(BF16)
                copy = remote(
                    ret_out.at[at], ret_in.at[my * cap + c],
                    ret_send.at[at], ret_recv.at[at], mx, src,
                )
                copy.start()
                returns.append(copy)

    work(my, 0)
    pass_on(0)
    wait_big(1, 0)
    wait_big(1, 1)
    for copy in stats:
        copy.wait_recv()
    work(sib, 1)
    pass_on(1)

    for copy in cols:
        copy.wait_recv()
    total = col_all[0]
    for d in range(1, n):
        total = total + col_all[d]
    row_sum[...] = total
    row_all[mx] = total

    def row_copy(t):
        return remote(row_sum, row_all.at[mx], row_send.at[t], row_recv.at[t], xpeer(t), my)

    def send_row(t, carry):
        row_copy(t).start()
        return carry

    lax.fori_loop(1, nx, send_row, 0)

    for t in range(1, half):
        work(lax.rem(my + n - 2 * t, n), 1 + t)
    for t in range(1, half):
        wait_big(half + t, 0)
        wait_big(half + t, 1)
        work(lax.rem(sib + n - 2 * t, n), half + t)

    for b in range(rb):
        dk = dk_acc[b]
        dv = dv_acc[b]
        for at in range(n * cap):
            hit = jnp.full((BLOCK, f), keyed[at], jnp.int32) == b
            dk = dk + jnp.where(hit, dk_part[at], 0.0)
            dv = dv + jnp.where(hit, dv_part[at], 0.0)
        dk_ref[b * BLOCK:(b + 1) * BLOCK] = dk.astype(BF16)
        dv_ref[b * BLOCK:(b + 1) * BLOCK] = dv.astype(BF16)

    stores = [
        pltpu.make_async_copy(src, dst, store_sem.at[at])
        for at, (src, dst) in enumerate(
            [(dk_ref, dk_hbm), (dv_ref, dv_hbm), (sg_ref, sg_hbm), (dq_ref, dq_hbm)]
        )
    ]
    stores[0].start()
    stores[1].start()

    def get_row(t, carry):
        row_copy(t).wait_recv()
        return carry

    lax.fori_loop(1, nx, get_row, 0)
    total = lax.fori_loop(1, nx, lambda d, acc: acc + row_all[d], row_all[0])
    sg_ref[...] = total / math.sqrt(pts * nx * n)

    stores[2].start()

    for copy in returns:
        copy.wait_recv()
    place = []
    for r in range(rb):
        for j in range(listed):
            value = nb_s[my, r, j]
            place.append(lax.div(value, rb))
    for r in range(rb):
        dqt = dq_acc[r]
        for j in range(listed):
            e = r * listed + j
            rank = jnp.int32(0)
            for before in range(e):
                rank = rank + (place[before] == place[e]).astype(jnp.int32)
            dqt = dqt + ret_in[place[e] * cap + rank].astype(F32)
        dq_ref[r * BLOCK:(r + 1) * BLOCK] = dqt.T.astype(BF16)

    stores[3].start()
    for copy in stores:
        copy.wait()
    for copy in halo + lists + stats + big + cols + forwards + returns:
        copy.wait_send()

    def end_row(t, carry):
        row_copy(t).wait_send()
        return carry

    lax.fori_loop(1, nx, end_row, 0)


def write(dq_ref, dk_ref, dv_ref, sg_ref, dq_hbm, dk_hbm, dv_hbm, sg_hbm, sems):
    copies = [
        pltpu.make_async_copy(src, dst, sems.at[at])
        for at, (src, dst) in enumerate(
            [(dq_ref, dq_hbm), (dk_ref, dk_hbm), (dv_ref, dv_hbm), (sg_ref, sg_hbm)]
        )
    ]
    for copy in copies:
        copy.start()
    for copy in copies:
        copy.wait()


def per_device(nx, n, queries, keys, values, out_attn, out_grad, log_norm, neighbour_blocks, stencil):
    tx, ty, f = queries.shape
    pts = tx * ty
    rb = pts // BLOCK
    listed = neighbour_blocks.shape[2]
    cap = max(2, (rb * listed + n - 1) // n)
    flat = [a.reshape(rb, BLOCK, f) for a in (queries, keys, values, out_attn, out_grad)]
    vmem = pl.BlockSpec(memory_space=pltpu.VMEM)
    hbm = pl.BlockSpec(memory_space=pltpu.HBM)
    flat_buf = pltpu.VMEM((pts, f), BF16)
    block_buf = pltpu.VMEM((rb, BLOCK, f), BF16)
    half = n // 2
    dma = pltpu.SemaphoreType.DMA
    grads = jax.ShapeDtypeStruct((pts, f), BF16)
    dq, dk, dv, sg = pl.pallas_call(
        functools.partial(kernel, nx, n, tx, ty, rb, listed, cap),
        out_shape=[grads, grads, grads, jax.ShapeDtypeStruct((8, f), F32)],
        in_specs=[hbm] * 7 + [vmem],
        out_specs=[hbm] * 4,
        scratch_shapes=[
            flat_buf, flat_buf, flat_buf, pltpu.VMEM((8, f), F32), dma((4,)),
            block_buf, block_buf, block_buf, block_buf, block_buf,
            pltpu.VMEM(log_norm.shape, BF16),
            pltpu.VMEM(stencil.shape, F32),
            dma((7,)),
            [pltpu.VMEM((rb, BLOCK, f), BF16)] * (n - 1),
            [pltpu.VMEM((rb, BLOCK, f), BF16)] * (n - 1),
            pltpu.VMEM((rb, 2 * HEADS, BLOCK), F32),
            pltpu.VMEM((n, rb, 2 * HEADS, BLOCK), F32),
            pltpu.VMEM((n, 8, 128), jnp.int32),
            pltpu.VMEM((8, 128), jnp.int32),
            pltpu.SMEM((n, 8, 128), jnp.int32),
            pltpu.VMEM((rb, f, HEADS * BLOCK), BF16),
            pltpu.VMEM((2, tx, f), BF16),
            pltpu.VMEM((2, ty, f), BF16),
            pltpu.VMEM((2, tx, f), BF16),
            pltpu.VMEM((rb, f, BLOCK), F32),
            pltpu.VMEM((rb, BLOCK, f), F32),
            pltpu.VMEM((rb, BLOCK, f), F32),
            pltpu.VMEM((n * cap, BLOCK, f), F32),
            pltpu.VMEM((n * cap, BLOCK, f), F32),
            pltpu.VMEM((n * cap, f, BLOCK), BF16),
            pltpu.VMEM((n * cap, f, BLOCK), BF16),
            pltpu.VMEM((8, f), F32),
            pltpu.VMEM((n, 8, f), F32),
            pltpu.VMEM((8, f), F32),
            pltpu.VMEM((nx, 8, f), F32),
            dma((n, 2)), dma((n, 2)),
            dma((n, 2)), dma((n, 2)),
            dma((4,)), dma((4,)),
            dma((n * cap,)), dma((n * cap,)),
            dma((n,)), dma((n,)),
            dma((nx,)), dma((nx,)),
            dma,
        ],
        compiler_params=pltpu.CompilerParams(
            collective_id=0, has_side_effects=True, vmem_limit_bytes=56 * 1024 * 1024
        ),
    )(*flat, log_norm, stencil, neighbour_blocks)
    dq, dk, dv, sg = pl.pallas_call(
        write,
        out_shape=[grads, grads, grads, jax.ShapeDtypeStruct((8, f), F32)],
        in_specs=[hbm] * 4,
        out_specs=[hbm] * 4,
        scratch_shapes=[dma((4,))],
        compiler_params=pltpu.CompilerParams(vmem_limit_bytes=56 * 1024 * 1024),
    )(dq, dk, dv, sg)
    shape = (tx, ty, f)
    return dq.reshape(shape), dk.reshape(shape), dv.reshape(shape), sg[:5]


def solution(mesh):
    placed = (
        P("gx", "gy", None),
        P("gx", "gy", None),
        P("gx", "gy", None),
        P("gx", "gy", None),
        P("gx", "gy", None),
        P(None, "gx", "gy"),
        P("gx", "gy", None),
        P(),
    )
    return jax.shard_map(
        functools.partial(per_device, mesh.shape["gx"], mesh.shape["gy"]),
        mesh=mesh,
        in_specs=placed,
        out_specs=(P("gx", "gy", None), P("gx", "gy", None), P("gx", "gy", None), P()),
        check_vma=False,
    )
```

```python
import functools
import math

import jax
import jax.numpy as jnp
from jax import lax
from jax.experimental import pallas as pl
from jax.experimental.pallas import tpu as pltpu
from jax.sharding import PartitionSpec as P

BLOCK = 128
HEADS = 4
LOG2E = 1.4426950408889634
F32 = jnp.float32
BF16 = jnp.bfloat16


def dot(a, b):
    return jnp.dot(a, b, preferred_element_type=F32)


def dot_nt(a, b):
    return lax.dot_general(a, b, (((1,), (1,)), ((), ())), preferred_element_type=F32)


def iota(shape, dim):
    return lax.broadcasted_iota(jnp.int32, shape, dim)


def kernel(
    nx, n, tx, ty, rb, listed, cap,
    q_hbm, k_hbm, v_hbm, o_hbm, g_hbm, ln_hbm, w_hbm, nb_hbm,
    dq_hbm, dk_hbm, dv_hbm, sg_hbm,
    dq_ref, dk_ref, dv_ref, sg_ref, store_sem,
    q_ref, k_ref, v_ref, o_ref, g_ref, ln_ref, w_ref, nb_ref, load_sem,
    q_in, g_in, st_own, st_all, nb_all, nb_own, nb_s, kmt, edge, xh, yh,
    dq_acc, dk_acc, dv_acc, dk_part, dv_part, ret_out, ret_in,
    part, col_all, row_sum, row_all,
    big_send, big_recv, small_send, small_recv, halo_send, halo_recv,
    ret_send, ret_recv, col_send, col_recv, row_send, row_recv, local_sem,
):
    nb_load, g_load, o_load, ln_load, k_load, v_load, q_load, w_load = [
        pltpu.make_async_copy(src, dst, load_sem.at[at])
        for at, (src, dst) in enumerate([
            (nb_hbm, nb_ref), (g_hbm, g_ref), (o_hbm, o_ref), (ln_hbm, ln_ref), (k_hbm, k_ref),
            (v_hbm, v_ref), (q_hbm, q_ref), (w_hbm, w_ref),
        ])
    ]
    f = q_ref.shape[2]
    pts = rb * BLOCK
    hw = f // HEADS
    scale = 1.0 / math.sqrt(hw)
    mx = lax.axis_index("gx")
    my = lax.axis_index("gy")
    half = n // 2
    sib = my + 1 - 2 * lax.rem(my, 2)

    def peer(t):
        return lax.rem(my + t, n)

    def xpeer(t):
        return lax.rem(mx + t, nx)

    barrier = pltpu.get_barrier_semaphore()
    for t in range(1, n):
        pl.semaphore_signal(barrier, inc=1, device_id=(mx, peer(t)), device_id_type=pl.DeviceIdType.MESH)

    def greet(t, carry):
        pl.semaphore_signal(barrier, inc=1, device_id=(xpeer(t), my), device_id_type=pl.DeviceIdType.MESH)
        return carry

    lax.fori_loop(1, nx, greet, 0)

    def remote(src, dst, ssem, rsem, x, y):
        return pltpu.make_async_remote_copy(
            src_ref=src, dst_ref=dst, send_sem=ssem, recv_sem=rsem,
            device_id=(x, y), device_id_type=pl.DeviceIdType.MESH,
        )

    for copy in (nb_load, g_load, o_load, ln_load, k_load, v_load, q_load, w_load):
        copy.start()
    nb_own[...] = jnp.zeros_like(nb_own)
    nb_load.wait()
    nb_own[0:listed, 0:rb] = nb_ref[...].reshape(listed, rb)
    pl.semaphore_wait(barrier, n - 1 + nx - 1)

    lists = [
        remote(nb_own, nb_all.at[my], small_send.at[t, 0], small_recv.at[t, 0], mx, peer(t))
        for t in range(1, n)
    ]
    big = []

    def send_big(t, which):
        to = sib if t == 0 else peer(2 * t)
        src, dst = ((q_hbm, q_in), (g_hbm, g_in))[which]
        big.append(remote(
            src, dst[t], big_send.at[1 + t, which], big_recv.at[1 + t, which], mx, to
        ))
        big[-1].start()

    for copy in lists:
        copy.start()
    for t in range(1, half):
        send_big(t, 0)

    g_load.wait()
    o_load.wait()
    ln_load.wait()
    g2 = g_ref[...].reshape(pts, f)
    rows_of = iota((2 * tx, pts), 0)
    want = jnp.where(rows_of < tx, rows_of * ty, (rows_of - tx) * ty + ty - 1)
    pick = (iota((2 * tx, pts), 1) == want).astype(F32).astype(BF16)
    edge[...] = dot(pick, g2).astype(BF16).reshape(2, tx, f)

    prod = g2.astype(F32) * o_ref[...].reshape(pts, f).astype(F32)
    high = prod.astype(BF16)
    low = (prod - high.astype(F32)).astype(BF16)
    head_row = iota((2 * HEADS, f), 0) - HEADS
    summing = (iota((2 * HEADS, f), 1) // hw == head_row).astype(F32).astype(BF16)
    lines = BLOCK // ty
    ln = ln_ref[...].astype(F32).reshape(HEADS * tx, ty)
    ln = jnp.concatenate([ln] * lines, axis=1)
    ln = jnp.where(
        iota(ln.shape, 1) // ty == lax.rem(iota(ln.shape, 0), lines), ln, 0.0
    ).astype(BF16)
    gr = iota((rb * 2 * HEADS, HEADS * tx), 0)
    gc = iota((rb * 2 * HEADS, HEADS * tx), 1)
    gather = (
        (gc // tx == lax.rem(gr, 2 * HEADS)) & (lax.rem(gc, tx) // lines == gr // (2 * HEADS))
    ).astype(F32).astype(BF16)
    ln_rows = dot(gather, ln) * LOG2E
    for b in range(rb):
        sl = slice(b * BLOCK, (b + 1) * BLOCK)
        delta = dot_nt(summing, high[sl]) + dot_nt(summing, low[sl])
        delta = delta.astype(BF16).astype(F32)
        st_own[b] = ln_rows[b * 2 * HEADS:(b + 1) * 2 * HEADS] + delta

    halo = [
        remote(edge.at[0], yh.at[0], halo_send.at[0], halo_recv.at[0], mx, peer(n - 1)),
        remote(edge.at[1], yh.at[1], halo_send.at[1], halo_recv.at[1], mx, peer(1)),
        remote(g_ref.at[0, pl.ds(0, ty)], xh.at[0], halo_send.at[2], halo_recv.at[2], xpeer(nx - 1), my),
        remote(g_ref.at[rb - 1, pl.ds(BLOCK - ty, ty)], xh.at[1], halo_send.at[3], halo_recv.at[3], xpeer(1), my),
    ]
    stats = [
        remote(st_own, st_all.at[my], small_send.at[t, 1], small_recv.at[t, 1], mx, peer(t))
        for t in range(1, n)
    ]
    for copy in halo + stats:
        copy.start()
    for t in range(1, half):
        send_big(t, 1)
    send_big(0, 0)
    send_big(0, 1)

    def wait_big(number, which):
        ref = (q_in, g_in)[which][number - 1]
        remote(
            ref, ref, big_send.at[number, which], big_recv.at[number, which], mx, sib
        ).wait_recv()

    lane_head = iota((BLOCK, f), 1) // hw
    row_head = iota((f, BLOCK), 0) // hw

    def by_head(x):
        return [jnp.where(lane_head == h, x, jnp.zeros_like(x)) for h in range(HEADS)]

    def item(q, g, st, k, v, kt):
        qs, gs = by_head(q), by_head(g)
        probs, grads = [], []
        for h in range(HEADS):
            s = dot_nt(k, qs[h])
            dp = dot_nt(v, gs[h])
            p = jnp.exp2(s * (scale * LOG2E) - st[h:h + 1])
            d = p * (dp - st[HEADS + h:HEADS + h + 1])
            probs.append(p.astype(BF16))
            grads.append(d.astype(BF16))
        dv = dot(jnp.concatenate(probs, 1), jnp.concatenate(gs, 0))
        dk = dot(jnp.concatenate(grads, 1), jnp.concatenate(qs, 0)) * scale
        dqt = dot(kt, jnp.concatenate(grads, 0)) * scale
        return dqt, dk, dv

    for copy in (k_load, v_load, q_load, w_load):
        copy.wait()
    for b in range(rb):
        k = k_ref[b]
        ktr = k.astype(F32).T.astype(BF16)
        kt = jnp.concatenate(
            [jnp.where(row_head == h, ktr, jnp.zeros_like(ktr)) for h in range(HEADS)], 1
        )
        kmt[b] = kt
        dqt, dk, dv = item(q_ref[b], g_ref[b], st_own[b], k, v_ref[b], kt)
        dq_acc[b] = dqt
        dk_acc[b] = dk
        dv_acc[b] = dv

    for copy in halo:
        copy.wait_recv()
    g32 = g2.astype(F32)
    v32 = v_ref[...].reshape(pts, f).astype(F32)
    pr = iota((pts, tx), 0)
    pc = iota((pts, tx), 1)
    put_next = (pr == pc * ty + ty - 1).astype(F32).astype(BF16)
    put_prev = (pr == pc * ty).astype(F32).astype(BF16)
    ycol = lax.rem(iota((pts, f), 0), ty)
    y_next = jnp.where(ycol == ty - 1, dot(put_next, yh[0]), pltpu.roll(g32, pts - 1, 0))
    y_prev = jnp.where(ycol == 0, dot(put_prev, yh[1]), pltpu.roll(g32, 1, 0))
    x_next = jnp.concatenate([g32[ty:], xh[0].astype(F32)], 0)
    x_prev = jnp.concatenate([xh[1].astype(F32), g32[:-ty]], 0)
    part[...] = jnp.zeros_like(part)
    term = None
    for index, moved in enumerate([g32, x_next, x_prev, y_next, y_prev]):
        part[index:index + 1] = jnp.sum(moved * v32, axis=0, keepdims=True)
        scaled = w_ref[index:index + 1] * moved
        term = scaled if term is None else term + scaled
    for b in range(rb):
        dv_acc[b] += term[b * BLOCK:(b + 1) * BLOCK]

    cols = [
        remote(part, col_all.at[my], col_send.at[t], col_recv.at[t], mx, peer(t)) for t in range(1, n)
    ]
    for copy in cols:
        copy.start()
    col_all[my] = part[...]

    for copy in lists:
        copy.wait_recv()
    nb_all[my] = nb_own[...]
    to_smem = pltpu.make_async_copy(nb_all, nb_s, local_sem)
    to_smem.start()
    to_smem.wait()

    def slots(src):
        rows = [jnp.int32(0)] * cap
        inner = [jnp.int32(0)] * cap
        count = jnp.int32(0)
        for r in range(rb):
            for j in range(listed):
                value = nb_s[src, j, r]
                mine = lax.div(value, rb) == my
                for c in range(cap):
                    here = mine & (count == c)
                    rows[c] = jnp.where(here, r, rows[c])
                    inner[c] = jnp.where(here, lax.rem(value, rb), inner[c])
                count = count + mine.astype(jnp.int32)
        return rows, inner, count

    forwards = []

    def pass_on(which):
        for t in range(1, half):
            wait_big(1 + t, which)
            ref = (q_in, g_in)[which]
            copy = remote(
                ref[t], ref[half + t - 1],
                big_send.at[half + t, which], big_recv.at[half + t, which], mx, sib,
            )
            copy.start()
            forwards.append(copy)

    keyed = []
    returns = []

    def work(src, number):
        rows, inner, count = slots(src)
        own = number == 0
        q_from = q_ref if own else q_in[number - 1]
        g_from = g_ref if own else g_in[number - 1]
        for c in range(cap):
            at = number * cap + c
            r, i = rows[c], inner[c]
            q, g = q_from[r], g_from[r]
            st = st_own[r] if own else st_all[src, r]
            dqt, dk, dv = item(q, g, st, k_ref[i], v_ref[i], kmt[i])
            dk_part[at] = dk
            dv_part[at] = dv
            keyed.append(jnp.where(count > c, i, -1))
            if own:
                ret_in[my * cap + c] = dqt.astype(BF16)
            else:
                ret_out[at] = dqt.astype(BF16)
                copy = remote(
                    ret_out.at[at], ret_in.at[my * cap + c],
                    ret_send.at[at], ret_recv.at[at], mx, src,
                )
                copy.start()
                returns.append(copy)

    work(my, 0)
    pass_on(0)
    wait_big(1, 0)
    wait_big(1, 1)
    for copy in stats:
        copy.wait_recv()
    work(sib, 1)
    pass_on(1)

    for copy in cols:
        copy.wait_recv()
    total = col_all[0]
    for d in range(1, n):
        total = total + col_all[d]
    row_sum[...] = total
    row_all[mx] = total

    def row_copy(t):
        return remote(row_sum, row_all.at[mx], row_send.at[t], row_recv.at[t], xpeer(t), my)

    def send_row(t, carry):
        row_copy(t).start()
        return carry

    lax.fori_loop(1, nx, send_row, 0)

    for t in range(1, half):
        work(lax.rem(my + n - 2 * t, n), 1 + t)
    for t in range(1, half):
        wait_big(half + t, 0)
        wait_big(half + t, 1)
        work(lax.rem(sib + n - 2 * t, n), half + t)

    for b in range(rb):
        dk = dk_acc[b]
        dv = dv_acc[b]
        for at in range(n * cap):
            hit = jnp.full((BLOCK, f), keyed[at], jnp.int32) == b
            dk = dk + jnp.where(hit, dk_part[at], 0.0)
            dv = dv + jnp.where(hit, dv_part[at], 0.0)
        dk_ref[b * BLOCK:(b + 1) * BLOCK] = dk.astype(BF16)
        dv_ref[b * BLOCK:(b + 1) * BLOCK] = dv.astype(BF16)

    stores = [
        pltpu.make_async_copy(src, dst, store_sem.at[at])
        for at, (src, dst) in enumerate(
            [(dk_ref, dk_hbm), (dv_ref, dv_hbm), (sg_ref, sg_hbm), (dq_ref, dq_hbm)]
        )
    ]
    stores[0].start()
    stores[1].start()

    def get_row(t, carry):
        row_copy(t).wait_recv()
        return carry

    lax.fori_loop(1, nx, get_row, 0)
    total = lax.fori_loop(1, nx, lambda d, acc: acc + row_all[d], row_all[0])
    sg_ref[...] = total / math.sqrt(pts * nx * n)

    stores[2].start()

    for copy in returns:
        copy.wait_recv()
    place = []
    for r in range(rb):
        for j in range(listed):
            value = nb_s[my, j, r]
            place.append(lax.div(value, rb))
    for r in range(rb):
        dqt = dq_acc[r]
        for j in range(listed):
            e = r * listed + j
            rank = jnp.int32(0)
            for before in range(e):
                rank = rank + (place[before] == place[e]).astype(jnp.int32)
            dqt = dqt + ret_in[place[e] * cap + rank].astype(F32)
        dq_ref[r * BLOCK:(r + 1) * BLOCK] = dqt.T.astype(BF16)

    stores[3].start()
    for copy in stores:
        copy.wait()
    for copy in halo + lists + stats + big + cols + forwards + returns:
        copy.wait_send()

    def end_row(t, carry):
        row_copy(t).wait_send()
        return carry

    lax.fori_loop(1, nx, end_row, 0)


def write(dq_in, dk_in, dv_in, sg_in, dq_hbm, dk_hbm, dv_hbm, sg_hbm, dq, dk, dv, sg, sems):
    loads, stores = [
        [
            pltpu.make_async_copy(src, dst, sems.at[way, at])
            for at, (src, dst) in enumerate(pairs)
        ]
        for way, pairs in enumerate([
            [(dk_in, dk), (dv_in, dv), (dq_in, dq), (sg_in, sg)],
            [(dk, dk_hbm), (dv, dv_hbm), (dq, dq_hbm), (sg, sg_hbm)],
        ])
    ]
    for copy in loads:
        copy.start()
    for load, store in zip(loads, stores):
        load.wait()
        store.start()
    for copy in stores:
        copy.wait()


def per_device(nx, n, queries, keys, values, out_attn, out_grad, log_norm, neighbour_blocks, stencil):
    tx, ty, f = queries.shape
    pts = tx * ty
    rb = pts // BLOCK
    listed = neighbour_blocks.shape[2]
    cap = max(2, (rb * listed + n - 1) // n)
    flat = [a.reshape(rb, BLOCK, f) for a in (queries, keys, values, out_attn, out_grad)]
    hbm = pl.BlockSpec(memory_space=pltpu.HBM)
    flat_buf = pltpu.VMEM((pts, f), BF16)
    block_buf = pltpu.VMEM((rb, BLOCK, f), BF16)
    half = n // 2
    dma = pltpu.SemaphoreType.DMA
    grads = jax.ShapeDtypeStruct((pts, f), BF16)
    dq, dk, dv, sg = pl.pallas_call(
        functools.partial(kernel, nx, n, tx, ty, rb, listed, cap),
        out_shape=[grads, grads, grads, jax.ShapeDtypeStruct((8, f), F32)],
        in_specs=[hbm] * 8,
        out_specs=[hbm] * 4,
        scratch_shapes=[
            flat_buf, flat_buf, flat_buf, pltpu.VMEM((8, f), F32), dma((4,)),
            block_buf, block_buf, block_buf, block_buf, block_buf,
            pltpu.VMEM(log_norm.shape, BF16),
            pltpu.VMEM(stencil.shape, F32),
            pltpu.VMEM((listed, 1, rb), jnp.int32),
            dma((8,)),
            [pltpu.VMEM((rb, BLOCK, f), BF16)] * (n - 1),
            [pltpu.VMEM((rb, BLOCK, f), BF16)] * (n - 1),
            pltpu.VMEM((rb, 2 * HEADS, BLOCK), F32),
            pltpu.VMEM((n, rb, 2 * HEADS, BLOCK), F32),
            pltpu.VMEM((n, 8, 128), jnp.int32),
            pltpu.VMEM((8, 128), jnp.int32),
            pltpu.SMEM((n, 8, 128), jnp.int32),
            pltpu.VMEM((rb, f, HEADS * BLOCK), BF16),
            pltpu.VMEM((2, tx, f), BF16),
            pltpu.VMEM((2, ty, f), BF16),
            pltpu.VMEM((2, tx, f), BF16),
            pltpu.VMEM((rb, f, BLOCK), F32),
            pltpu.VMEM((rb, BLOCK, f), F32),
            pltpu.VMEM((rb, BLOCK, f), F32),
            pltpu.VMEM((n * cap, BLOCK, f), F32),
            pltpu.VMEM((n * cap, BLOCK, f), F32),
            pltpu.VMEM((n * cap, f, BLOCK), BF16),
            pltpu.VMEM((n * cap, f, BLOCK), BF16),
            pltpu.VMEM((8, f), F32),
            pltpu.VMEM((n, 8, f), F32),
            pltpu.VMEM((8, f), F32),
            pltpu.VMEM((nx, 8, f), F32),
            dma((n, 2)), dma((n, 2)),
            dma((n, 2)), dma((n, 2)),
            dma((4,)), dma((4,)),
            dma((n * cap,)), dma((n * cap,)),
            dma((n,)), dma((n,)),
            dma((nx,)), dma((nx,)),
            dma,
        ],
        compiler_params=pltpu.CompilerParams(
            collective_id=0, has_side_effects=True, vmem_limit_bytes=56 * 1024 * 1024
        ),
    )(*flat, log_norm, stencil, neighbour_blocks.transpose(2, 0, 1))
    dq, dk, dv, sg = pl.pallas_call(
        write,
        out_shape=[grads, grads, grads, jax.ShapeDtypeStruct((8, f), F32)],
        in_specs=[hbm] * 4,
        out_specs=[hbm] * 4,
        scratch_shapes=[flat_buf, flat_buf, flat_buf, pltpu.VMEM((8, f), F32), dma((2, 4))],
        compiler_params=pltpu.CompilerParams(vmem_limit_bytes=56 * 1024 * 1024),
    )(dq, dk, dv, sg)
    shape = (tx, ty, f)
    return dq.reshape(shape), dk.reshape(shape), dv.reshape(shape), sg[:5]


def solution(mesh):
    placed = (
        P("gx", "gy", None),
        P("gx", "gy", None),
        P("gx", "gy", None),
        P("gx", "gy", None),
        P("gx", "gy", None),
        P(None, "gx", "gy"),
        P("gx", "gy", None),
        P(),
    )
    return jax.shard_map(
        functools.partial(per_device, mesh.shape["gx"], mesh.shape["gy"]),
        mesh=mesh,
        in_specs=placed,
        out_specs=(P("gx", "gy", None), P("gx", "gy", None), P("gx", "gy", None), P()),
        check_vma=False,
    )
```

```python
import functools
import math

import jax
import jax.numpy as jnp
from jax import lax
from jax.experimental import pallas as pl
from jax.experimental.pallas import tpu as pltpu
from jax.sharding import PartitionSpec as P

BLOCK = 128
HEADS = 4
LOG2E = 1.4426950408889634
F32 = jnp.float32
BF16 = jnp.bfloat16


def dot(a, b):
    return jnp.dot(a, b, preferred_element_type=F32)


def dot_nt(a, b):
    return lax.dot_general(a, b, (((1,), (1,)), ((), ())), preferred_element_type=F32)


def iota(shape, dim):
    return lax.broadcasted_iota(jnp.int32, shape, dim)


def kernel(
    nx, n, tx, ty, rb, listed, cap,
    q_hbm, k_hbm, v_hbm, o_hbm, g_hbm, ln_hbm, w_hbm, nb_hbm,
    dq_ref, dk_ref, dv_ref, sg_ref,
    q_ref, k_ref, v_ref, o_ref, g_ref, ln_ref, w_ref, nb_ref, load_sem,
    q_in, g_in, st_own, st_all, nb_all, nb_own, nb_s, kmt, edge, xh, yh,
    dq_acc, dk_acc, dv_acc, dk_part, dv_part, ret_out, ret_in,
    part, col_all, row_sum, row_all,
    big_send, big_recv, small_send, small_recv, halo_send, halo_recv,
    ret_send, ret_recv, col_send, col_recv, row_send, row_recv, local_sem,
):
    nb_load, g_load, o_load, ln_load, k_load, v_load, q_load, w_load = [
        pltpu.make_async_copy(src, dst, load_sem.at[at])
        for at, (src, dst) in enumerate([
            (nb_hbm, nb_ref), (g_hbm, g_ref), (o_hbm, o_ref), (ln_hbm, ln_ref), (k_hbm, k_ref),
            (v_hbm, v_ref), (q_hbm, q_ref), (w_hbm, w_ref),
        ])
    ]
    f = q_ref.shape[2]
    pts = rb * BLOCK
    hw = f // HEADS
    scale = 1.0 / math.sqrt(hw)
    mx = lax.axis_index("gx")
    my = lax.axis_index("gy")
    half = n // 2
    sib = my + 1 - 2 * lax.rem(my, 2)

    def peer(t):
        return lax.rem(my + t, n)

    def xpeer(t):
        return lax.rem(mx + t, nx)

    barrier = pltpu.get_barrier_semaphore()
    for t in range(1, n):
        pl.semaphore_signal(barrier, inc=1, device_id=(mx, peer(t)), device_id_type=pl.DeviceIdType.MESH)

    def greet(t, carry):
        pl.semaphore_signal(barrier, inc=1, device_id=(xpeer(t), my), device_id_type=pl.DeviceIdType.MESH)
        return carry

    lax.fori_loop(1, nx, greet, 0)

    def remote(src, dst, ssem, rsem, x, y):
        return pltpu.make_async_remote_copy(
            src_ref=src, dst_ref=dst, send_sem=ssem, recv_sem=rsem,
            device_id=(x, y), device_id_type=pl.DeviceIdType.MESH,
        )

    for copy in (nb_load, g_load, o_load, ln_load, k_load, v_load, q_load, w_load):
        copy.start()
    nb_own[...] = jnp.zeros_like(nb_own)
    nb_load.wait()
    nb_own[0:listed, 0:rb] = nb_ref[...].reshape(listed, rb)
    pl.semaphore_wait(barrier, n - 1 + nx - 1)

    lists = [
        remote(nb_own, nb_all.at[my], small_send.at[t, 0], small_recv.at[t, 0], mx, peer(t))
        for t in range(1, n)
    ]
    big = []

    def send_big(t, which):
        to = sib if t == 0 else peer(2 * t)
        src, dst = ((q_hbm, q_in), (g_hbm, g_in))[which]
        big.append(remote(
            src, dst[t], big_send.at[1 + t, which], big_recv.at[1 + t, which], mx, to
        ))
        big[-1].start()

    for copy in lists:
        copy.start()
    for t in range(1, half):
        send_big(t, 0)

    g_load.wait()
    o_load.wait()
    ln_load.wait()
    g2 = g_ref[...].reshape(pts, f)
    rows_of = iota((2 * tx, pts), 0)
    want = jnp.where(rows_of < tx, rows_of * ty, (rows_of - tx) * ty + ty - 1)
    pick = (iota((2 * tx, pts), 1) == want).astype(F32).astype(BF16)
    edge[...] = dot(pick, g2).astype(BF16).reshape(2, tx, f)

    prod = g2.astype(F32) * o_ref[...].reshape(pts, f).astype(F32)
    high = prod.astype(BF16)
    low = (prod - high.astype(F32)).astype(BF16)
    head_row = iota((2 * HEADS, f), 0) - HEADS
    summing = (iota((2 * HEADS, f), 1) // hw == head_row).astype(F32).astype(BF16)
    lines = BLOCK // ty
    ln = ln_ref[...].astype(F32).reshape(HEADS * tx, ty)
    ln = jnp.concatenate([ln] * lines, axis=1)
    ln = jnp.where(
        iota(ln.shape, 1) // ty == lax.rem(iota(ln.shape, 0), lines), ln, 0.0
    ).astype(BF16)
    gr = iota((rb * 2 * HEADS, HEADS * tx), 0)
    gc = iota((rb * 2 * HEADS, HEADS * tx), 1)
    gather = (
        (gc // tx == lax.rem(gr, 2 * HEADS)) & (lax.rem(gc, tx) // lines == gr // (2 * HEADS))
    ).astype(F32).astype(BF16)
    ln_rows = dot(gather, ln) * LOG2E
    for b in range(rb):
        sl = slice(b * BLOCK, (b + 1) * BLOCK)
        delta = dot_nt(summing, high[sl]) + dot_nt(summing, low[sl])
        delta = delta.astype(BF16).astype(F32)
        st_own[b] = ln_rows[b * 2 * HEADS:(b + 1) * 2 * HEADS] + delta

    halo = [
        remote(edge.at[0], yh.at[0], halo_send.at[0], halo_recv.at[0], mx, peer(n - 1)),
        remote(edge.at[1], yh.at[1], halo_send.at[1], halo_recv.at[1], mx, peer(1)),
        remote(g_ref.at[0, pl.ds(0, ty)], xh.at[0], halo_send.at[2], halo_recv.at[2], xpeer(nx - 1), my),
        remote(g_ref.at[rb - 1, pl.ds(BLOCK - ty, ty)], xh.at[1], halo_send.at[3], halo_recv.at[3], xpeer(1), my),
    ]
    stats = [
        remote(st_own, st_all.at[my], small_send.at[t, 1], small_recv.at[t, 1], mx, peer(t))
        for t in range(1, n)
    ]
    for copy in halo + stats:
        copy.start()
    for t in range(1, half):
        send_big(t, 1)
    send_big(0, 0)
    send_big(0, 1)

    def wait_big(number, which):
        ref = (q_in, g_in)[which][number - 1]
        remote(
            ref, ref, big_send.at[number, which], big_recv.at[number, which], mx, sib
        ).wait_recv()

    lane_head = iota((BLOCK, f), 1) // hw
    row_head = iota((f, BLOCK), 0) // hw

    def by_head(x):
        return [jnp.where(lane_head == h, x, jnp.zeros_like(x)) for h in range(HEADS)]

    def item(q, g, st, k, v, kt):
        qs, gs = by_head(q), by_head(g)
        probs, grads = [], []
        for h in range(HEADS):
            s = dot_nt(k, qs[h])
            dp = dot_nt(v, gs[h])
            p = jnp.exp2(s * (scale * LOG2E) - st[h:h + 1])
            d = p * (dp - st[HEADS + h:HEADS + h + 1])
            probs.append(p.astype(BF16))
            grads.append(d.astype(BF16))
        dv = dot(jnp.concatenate(probs, 1), jnp.concatenate(gs, 0))
        dk = dot(jnp.concatenate(grads, 1), jnp.concatenate(qs, 0)) * scale
        dqt = dot(kt, jnp.concatenate(grads, 0)) * scale
        return dqt, dk, dv

    for copy in (k_load, v_load, q_load, w_load):
        copy.wait()
    for b in range(rb):
        k = k_ref[b]
        ktr = k.astype(F32).T.astype(BF16)
        kt = jnp.concatenate(
            [jnp.where(row_head == h, ktr, jnp.zeros_like(ktr)) for h in range(HEADS)], 1
        )
        kmt[b] = kt
        dqt, dk, dv = item(q_ref[b], g_ref[b], st_own[b], k, v_ref[b], kt)
        dq_acc[b] = dqt
        dk_acc[b] = dk
        dv_acc[b] = dv

    for copy in halo:
        copy.wait_recv()
    g32 = g2.astype(F32)
    v32 = v_ref[...].reshape(pts, f).astype(F32)
    pr = iota((pts, tx), 0)
    pc = iota((pts, tx), 1)
    put_next = (pr == pc * ty + ty - 1).astype(F32).astype(BF16)
    put_prev = (pr == pc * ty).astype(F32).astype(BF16)
    ycol = lax.rem(iota((pts, f), 0), ty)
    y_next = jnp.where(ycol == ty - 1, dot(put_next, yh[0]), pltpu.roll(g32, pts - 1, 0))
    y_prev = jnp.where(ycol == 0, dot(put_prev, yh[1]), pltpu.roll(g32, 1, 0))
    x_next = jnp.concatenate([g32[ty:], xh[0].astype(F32)], 0)
    x_prev = jnp.concatenate([xh[1].astype(F32), g32[:-ty]], 0)
    part[...] = jnp.zeros_like(part)
    term = None
    for index, moved in enumerate([g32, x_next, x_prev, y_next, y_prev]):
        part[index:index + 1] = jnp.sum(moved * v32, axis=0, keepdims=True)
        scaled = w_ref[index:index + 1] * moved
        term = scaled if term is None else term + scaled
    for b in range(rb):
        dv_acc[b] += term[b * BLOCK:(b + 1) * BLOCK]

    cols = [
        remote(part, col_all.at[my], col_send.at[t], col_recv.at[t], mx, peer(t)) for t in range(1, n)
    ]
    for copy in cols:
        copy.start()
    col_all[my] = part[...]

    for copy in lists:
        copy.wait_recv()
    nb_all[my] = nb_own[...]
    to_smem = pltpu.make_async_copy(nb_all, nb_s, local_sem)
    to_smem.start()
    to_smem.wait()

    def slots(src):
        rows = [jnp.int32(0)] * cap
        inner = [jnp.int32(0)] * cap
        count = jnp.int32(0)
        for r in range(rb):
            for j in range(listed):
                value = nb_s[src, j, r]
                mine = lax.div(value, rb) == my
                for c in range(cap):
                    here = mine & (count == c)
                    rows[c] = jnp.where(here, r, rows[c])
                    inner[c] = jnp.where(here, lax.rem(value, rb), inner[c])
                count = count + mine.astype(jnp.int32)
        return rows, inner, count

    forwards = []

    def pass_on(which):
        for t in range(1, half):
            wait_big(1 + t, which)
            ref = (q_in, g_in)[which]
            copy = remote(
                ref[t], ref[half + t - 1],
                big_send.at[half + t, which], big_recv.at[half + t, which], mx, sib,
            )
            copy.start()
            forwards.append(copy)

    keyed = []
    returns = []

    def work(src, number):
        rows, inner, count = slots(src)
        own = number == 0
        q_from = q_ref if own else q_in[number - 1]
        g_from = g_ref if own else g_in[number - 1]
        for c in range(cap):
            at = number * cap + c
            r, i = rows[c], inner[c]
            q, g = q_from[r], g_from[r]
            st = st_own[r] if own else st_all[src, r]
            dqt, dk, dv = item(q, g, st, k_ref[i], v_ref[i], kmt[i])
            dk_part[at] = dk
            dv_part[at] = dv
            keyed.append(jnp.where(count > c, i, -1))
            if own:
                ret_in[my * cap + c] = dqt.astype(BF16)
            else:
                ret_out[at] = dqt.astype(BF16)
                copy = remote(
                    ret_out.at[at], ret_in.at[my * cap + c],
                    ret_send.at[at], ret_recv.at[at], mx, src,
                )
                copy.start()
                returns.append(copy)

    work(my, 0)
    pass_on(0)
    wait_big(1, 0)
    wait_big(1, 1)
    for copy in stats:
        copy.wait_recv()
    work(sib, 1)
    pass_on(1)

    for copy in cols:
        copy.wait_recv()
    total = col_all[0]
    for d in range(1, n):
        total = total + col_all[d]
    row_sum[...] = total
    row_all[mx] = total

    def row_copy(t):
        return remote(row_sum, row_all.at[mx], row_send.at[t], row_recv.at[t], xpeer(t), my)

    def send_row(t, carry):
        row_copy(t).start()
        return carry

    lax.fori_loop(1, nx, send_row, 0)

    for t in range(1, half):
        work(lax.rem(my + n - 2 * t, n), 1 + t)
    for t in range(1, half):
        wait_big(half + t, 0)
        wait_big(half + t, 1)
        work(lax.rem(sib + n - 2 * t, n), half + t)

    for b in range(rb):
        dk = dk_acc[b]
        dv = dv_acc[b]
        for at in range(n * cap):
            hit = jnp.full((BLOCK, f), keyed[at], jnp.int32) == b
            dk = dk + jnp.where(hit, dk_part[at], 0.0)
            dv = dv + jnp.where(hit, dv_part[at], 0.0)
        dk_ref[b * BLOCK:(b + 1) * BLOCK] = dk.astype(BF16)
        dv_ref[b * BLOCK:(b + 1) * BLOCK] = dv.astype(BF16)

    def get_row(t, carry):
        row_copy(t).wait_recv()
        return carry

    lax.fori_loop(1, nx, get_row, 0)
    total = lax.fori_loop(1, nx, lambda d, acc: acc + row_all[d], row_all[0])
    sg_ref[...] = total / math.sqrt(pts * nx * n)

    for copy in returns:
        copy.wait_recv()
    place = []
    for r in range(rb):
        for j in range(listed):
            value = nb_s[my, j, r]
            place.append(lax.div(value, rb))
    for r in range(rb):
        dqt = dq_acc[r]
        for j in range(listed):
            e = r * listed + j
            rank = jnp.int32(0)
            for before in range(e):
                rank = rank + (place[before] == place[e]).astype(jnp.int32)
            dqt = dqt + ret_in[place[e] * cap + rank].astype(F32)
        dq_ref[r * BLOCK:(r + 1) * BLOCK] = dqt.T.astype(BF16)

    for copy in halo + lists + stats + big + cols + forwards + returns:
        copy.wait_send()

    def end_row(t, carry):
        row_copy(t).wait_send()
        return carry

    lax.fori_loop(1, nx, end_row, 0)


def write(dq, dk, dv, sg, dq_hbm, dk_hbm, dv_hbm, sg_hbm, sems):
    copies = [
        pltpu.make_async_copy(src, dst, sems.at[at])
        for at, (src, dst) in enumerate(
            [(dq, dq_hbm), (dk, dk_hbm), (dv, dv_hbm), (sg, sg_hbm)]
        )
    ]
    for copy in copies:
        copy.start()
    for copy in copies:
        copy.wait()


def per_device(nx, n, queries, keys, values, out_attn, out_grad, log_norm, neighbour_blocks, stencil):
    tx, ty, f = queries.shape
    pts = tx * ty
    rb = pts // BLOCK
    listed = neighbour_blocks.shape[2]
    cap = max(2, (rb * listed + n - 1) // n)
    flat = [a.reshape(rb, BLOCK, f) for a in (queries, keys, values, out_attn, out_grad)]
    hbm = pl.BlockSpec(memory_space=pltpu.HBM)
    vmem = pl.BlockSpec(memory_space=pltpu.VMEM)
    block_buf = pltpu.VMEM((rb, BLOCK, f), BF16)
    half = n // 2
    dma = pltpu.SemaphoreType.DMA
    grads = jax.ShapeDtypeStruct((pts, f), BF16)
    dq, dk, dv, sg = pl.pallas_call(
        functools.partial(kernel, nx, n, tx, ty, rb, listed, cap),
        out_shape=[pltpu.VMEM((pts, f), BF16)] * 3 + [pltpu.VMEM((8, f), F32)],
        in_specs=[hbm] * 8,
        out_specs=[vmem] * 4,
        scratch_shapes=[
            block_buf, block_buf, block_buf, block_buf, block_buf,
            pltpu.VMEM(log_norm.shape, BF16),
            pltpu.VMEM(stencil.shape, F32),
            pltpu.VMEM((listed, 1, rb), jnp.int32),
            dma((8,)),
            [pltpu.VMEM((rb, BLOCK, f), BF16)] * (n - 1),
            [pltpu.VMEM((rb, BLOCK, f), BF16)] * (n - 1),
            pltpu.VMEM((rb, 2 * HEADS, BLOCK), F32),
            pltpu.VMEM((n, rb, 2 * HEADS, BLOCK), F32),
            pltpu.VMEM((n, 8, 128), jnp.int32),
            pltpu.VMEM((8, 128), jnp.int32),
            pltpu.SMEM((n, 8, 128), jnp.int32),
            pltpu.VMEM((rb, f, HEADS * BLOCK), BF16),
            pltpu.VMEM((2, tx, f), BF16),
            pltpu.VMEM((2, ty, f), BF16),
            pltpu.VMEM((2, tx, f), BF16),
            pltpu.VMEM((rb, f, BLOCK), F32),
            pltpu.VMEM((rb, BLOCK, f), F32),
            pltpu.VMEM((rb, BLOCK, f), F32),
            pltpu.VMEM((n * cap, BLOCK, f), F32),
            pltpu.VMEM((n * cap, BLOCK, f), F32),
            pltpu.VMEM((n * cap, f, BLOCK), BF16),
            pltpu.VMEM((n * cap, f, BLOCK), BF16),
            pltpu.VMEM((8, f), F32),
            pltpu.VMEM((n, 8, f), F32),
            pltpu.VMEM((8, f), F32),
            pltpu.VMEM((nx, 8, f), F32),
            dma((n, 2)), dma((n, 2)),
            dma((n, 2)), dma((n, 2)),
            dma((4,)), dma((4,)),
            dma((n * cap,)), dma((n * cap,)),
            dma((n,)), dma((n,)),
            dma((nx,)), dma((nx,)),
            dma,
        ],
        compiler_params=pltpu.CompilerParams(
            collective_id=0, has_side_effects=True, vmem_limit_bytes=56 * 1024 * 1024
        ),
    )(*flat, log_norm, stencil, neighbour_blocks.transpose(2, 0, 1))
    dq, dk, dv, sg = pl.pallas_call(
        write,
        out_shape=[grads, grads, grads, jax.ShapeDtypeStruct((8, f), F32)],
        in_specs=[vmem] * 4,
        out_specs=[hbm] * 4,
        scratch_shapes=[dma((4,))],
        compiler_params=pltpu.CompilerParams(vmem_limit_bytes=4 * 1024 * 1024),
    )(dq, dk, dv, sg)
    shape = (tx, ty, f)
    return dq.reshape(shape), dk.reshape(shape), dv.reshape(shape), sg[:5]


def solution(mesh):
    placed = (
        P("gx", "gy", None),
        P("gx", "gy", None),
        P("gx", "gy", None),
        P("gx", "gy", None),
        P("gx", "gy", None),
        P(None, "gx", "gy"),
        P("gx", "gy", None),
        P(),
    )
    return jax.shard_map(
        functools.partial(per_device, mesh.shape["gx"], mesh.shape["gy"]),
        mesh=mesh,
        in_specs=placed,
        out_specs=(P("gx", "gy", None), P("gx", "gy", None), P("gx", "gy", None), P()),
        check_vma=False,
    )
```

```python
import functools
import math

import jax
import jax.numpy as jnp
from jax import lax
from jax.experimental import pallas as pl
from jax.experimental.pallas import tpu as pltpu
from jax.sharding import PartitionSpec as P

BLOCK = 128
HEADS = 4
LOG2E = 1.4426950408889634
F32 = jnp.float32
BF16 = jnp.bfloat16


def dot(a, b):
    return jnp.dot(a, b, preferred_element_type=F32)


def dot_nt(a, b):
    return lax.dot_general(a, b, (((1,), (1,)), ((), ())), preferred_element_type=F32)


def iota(shape, dim):
    return lax.broadcasted_iota(jnp.int32, shape, dim)


def kernel(
    nx, n, tx, ty, rb, listed, cap,
    q_hbm, k_hbm, v_hbm, o_hbm, g_hbm, ln_hbm, w_hbm, nb_hbm,
    dq_ref, dk_ref, dv_ref, sg_ref,
    q_ref, k_ref, v_ref, o_ref, g_ref, ln_ref, w_ref, nb_ref, load_sem,
    q_in, g_in, st_own, st_all, nb_all, nb_own, nb_s, kmt, edge, xh, yh,
    dq_acc, dk_acc, dv_acc, dk_part, dv_part, ret_out, ret_in,
    part, col_all, row_sum, row_all,
    big_send, big_recv, small_send, small_recv, halo_send, halo_recv,
    ret_send, ret_recv, col_send, col_recv, row_send, row_recv, local_sem,
):
    nb_load, g_load, o_load, ln_load, k_load, v_load, q_load, w_load = [
        pltpu.make_async_copy(src, dst, load_sem.at[at])
        for at, (src, dst) in enumerate([
            (nb_hbm, nb_ref), (g_hbm, g_ref), (o_hbm, o_ref), (ln_hbm, ln_ref), (k_hbm, k_ref),
            (v_hbm, v_ref), (q_hbm, q_ref), (w_hbm, w_ref),
        ])
    ]
    f = q_ref.shape[2]
    pts = rb * BLOCK
    hw = f // HEADS
    scale = 1.0 / math.sqrt(hw)
    mx = lax.axis_index("gx")
    my = lax.axis_index("gy")
    half = n // 2
    sib = my + 1 - 2 * lax.rem(my, 2)

    def peer(t):
        return lax.rem(my + t, n)

    def xpeer(t):
        return lax.rem(mx + t, nx)

    barrier = pltpu.get_barrier_semaphore()
    for t in range(1, n):
        pl.semaphore_signal(barrier, inc=1, device_id=(mx, peer(t)), device_id_type=pl.DeviceIdType.MESH)

    def greet(t, carry):
        pl.semaphore_signal(barrier, inc=1, device_id=(xpeer(t), my), device_id_type=pl.DeviceIdType.MESH)
        return carry

    lax.fori_loop(1, nx, greet, 0)

    def remote(src, dst, ssem, rsem, x, y):
        return pltpu.make_async_remote_copy(
            src_ref=src, dst_ref=dst, send_sem=ssem, recv_sem=rsem,
            device_id=(x, y), device_id_type=pl.DeviceIdType.MESH,
        )

    for copy in (nb_load, g_load, o_load, ln_load, k_load, v_load, q_load, w_load):
        copy.start()
    nb_own[...] = jnp.zeros_like(nb_own)
    nb_load.wait()
    nb_own[0:listed, 0:rb] = nb_ref[...].reshape(listed, rb)
    pl.semaphore_wait(barrier, n - 1 + nx - 1)

    lists = [
        remote(nb_own, nb_all.at[my], small_send.at[t, 0], small_recv.at[t, 0], mx, peer(t))
        for t in range(1, n)
    ]
    big = []

    def send_big(t, which):
        to = sib if t == 0 else peer(2 * t)
        src, dst = ((q_hbm, q_in), (g_hbm, g_in))[which]
        big.append(remote(
            src, dst[t], big_send.at[1 + t, which], big_recv.at[1 + t, which], mx, to
        ))
        big[-1].start()

    for copy in lists:
        copy.start()
    for which in range(2):
        for t in range(1, half):
            send_big(t, which)

    g_load.wait()
    o_load.wait()
    ln_load.wait()
    g2 = g_ref[...].reshape(pts, f)
    rows_of = iota((2 * tx, pts), 0)
    want = jnp.where(rows_of < tx, rows_of * ty, (rows_of - tx) * ty + ty - 1)
    pick = (iota((2 * tx, pts), 1) == want).astype(F32).astype(BF16)
    edge[...] = dot(pick, g2).astype(BF16).reshape(2, tx, f)

    prod = g2.astype(F32) * o_ref[...].reshape(pts, f).astype(F32)
    high = prod.astype(BF16)
    low = (prod - high.astype(F32)).astype(BF16)
    head_row = iota((2 * HEADS, f), 0) - HEADS
    summing = (iota((2 * HEADS, f), 1) // hw == head_row).astype(F32).astype(BF16)
    lines = BLOCK // ty
    ln = ln_ref[...].astype(F32).reshape(HEADS * tx, ty)
    ln = jnp.concatenate([ln] * lines, axis=1)
    ln = jnp.where(
        iota(ln.shape, 1) // ty == lax.rem(iota(ln.shape, 0), lines), ln, 0.0
    ).astype(BF16)
    gr = iota((rb * 2 * HEADS, HEADS * tx), 0)
    gc = iota((rb * 2 * HEADS, HEADS * tx), 1)
    gather = (
        (gc // tx == lax.rem(gr, 2 * HEADS)) & (lax.rem(gc, tx) // lines == gr // (2 * HEADS))
    ).astype(F32).astype(BF16)
    ln_rows = dot(gather, ln) * LOG2E
    for b in range(rb):
        sl = slice(b * BLOCK, (b + 1) * BLOCK)
        delta = dot_nt(summing, high[sl]) + dot_nt(summing, low[sl])
        delta = delta.astype(BF16).astype(F32)
        st_own[b] = ln_rows[b * 2 * HEADS:(b + 1) * 2 * HEADS] + delta

    halo = [
        remote(edge.at[0], yh.at[0], halo_send.at[0], halo_recv.at[0], mx, peer(n - 1)),
        remote(edge.at[1], yh.at[1], halo_send.at[1], halo_recv.at[1], mx, peer(1)),
        remote(g_ref.at[0, pl.ds(0, ty)], xh.at[0], halo_send.at[2], halo_recv.at[2], xpeer(nx - 1), my),
        remote(g_ref.at[rb - 1, pl.ds(BLOCK - ty, ty)], xh.at[1], halo_send.at[3], halo_recv.at[3], xpeer(1), my),
    ]
    stats = [
        remote(st_own, st_all.at[my], small_send.at[t, 1], small_recv.at[t, 1], mx, peer(t))
        for t in range(1, n)
    ]
    for copy in halo + stats:
        copy.start()
    send_big(0, 0)
    send_big(0, 1)

    def wait_big(number, which):
        ref = (q_in, g_in)[which][number - 1]
        remote(
            ref, ref, big_send.at[number, which], big_recv.at[number, which], mx, sib
        ).wait_recv()

    lane_head = iota((BLOCK, f), 1) // hw
    row_head = iota((f, BLOCK), 0) // hw

    def by_head(x):
        return [jnp.where(lane_head == h, x, jnp.zeros_like(x)) for h in range(HEADS)]

    def item(q, g, st, k, v, kt):
        qs, gs = by_head(q), by_head(g)
        probs, grads = [], []
        for h in range(HEADS):
            s = dot_nt(k, qs[h])
            dp = dot_nt(v, gs[h])
            p = jnp.exp2(s * (scale * LOG2E) - st[h:h + 1])
            d = p * (dp - st[HEADS + h:HEADS + h + 1])
            probs.append(p.astype(BF16))
            grads.append(d.astype(BF16))
        dv = dot(jnp.concatenate(probs, 1), jnp.concatenate(gs, 0))
        dk = dot(jnp.concatenate(grads, 1), jnp.concatenate(qs, 0)) * scale
        dqt = dot(kt, jnp.concatenate(grads, 0)) * scale
        return dqt, dk, dv

    for copy in (k_load, v_load, q_load, w_load):
        copy.wait()
    for b in range(rb):
        k = k_ref[b]
        ktr = k.astype(F32).T.astype(BF16)
        kt = jnp.concatenate(
            [jnp.where(row_head == h, ktr, jnp.zeros_like(ktr)) for h in range(HEADS)], 1
        )
        kmt[b] = kt
        dqt, dk, dv = item(q_ref[b], g_ref[b], st_own[b], k, v_ref[b], kt)
        dq_acc[b] = dqt
        dk_acc[b] = dk
        dv_acc[b] = dv

    for copy in halo:
        copy.wait_recv()
    g32 = g2.astype(F32)
    v32 = v_ref[...].reshape(pts, f).astype(F32)
    pr = iota((pts, tx), 0)
    pc = iota((pts, tx), 1)
    put_next = (pr == pc * ty + ty - 1).astype(F32).astype(BF16)
    put_prev = (pr == pc * ty).astype(F32).astype(BF16)
    ycol = lax.rem(iota((pts, f), 0), ty)
    y_next = jnp.where(ycol == ty - 1, dot(put_next, yh[0]), pltpu.roll(g32, pts - 1, 0))
    y_prev = jnp.where(ycol == 0, dot(put_prev, yh[1]), pltpu.roll(g32, 1, 0))
    x_next = jnp.concatenate([g32[ty:], xh[0].astype(F32)], 0)
    x_prev = jnp.concatenate([xh[1].astype(F32), g32[:-ty]], 0)
    part[...] = jnp.zeros_like(part)
    term = None
    for index, moved in enumerate([g32, x_next, x_prev, y_next, y_prev]):
        part[index:index + 1] = jnp.sum(moved * v32, axis=0, keepdims=True)
        scaled = w_ref[index:index + 1] * moved
        term = scaled if term is None else term + scaled
    for b in range(rb):
        dv_acc[b] += term[b * BLOCK:(b + 1) * BLOCK]

    cols = [
        remote(part, col_all.at[my], col_send.at[t], col_recv.at[t], mx, peer(t)) for t in range(1, n)
    ]
    for copy in cols:
        copy.start()
    col_all[my] = part[...]

    for copy in lists:
        copy.wait_recv()
    nb_all[my] = nb_own[...]
    to_smem = pltpu.make_async_copy(nb_all, nb_s, local_sem)
    to_smem.start()
    to_smem.wait()

    def slots(src):
        rows = [jnp.int32(0)] * cap
        inner = [jnp.int32(0)] * cap
        count = jnp.int32(0)
        for r in range(rb):
            for j in range(listed):
                value = nb_s[src, j, r]
                mine = lax.div(value, rb) == my
                for c in range(cap):
                    here = mine & (count == c)
                    rows[c] = jnp.where(here, r, rows[c])
                    inner[c] = jnp.where(here, lax.rem(value, rb), inner[c])
                count = count + mine.astype(jnp.int32)
        return rows, inner, count

    forwards = []

    def pass_on(which):
        for t in range(1, half):
            wait_big(1 + t, which)
            ref = (q_in, g_in)[which]
            copy = remote(
                ref[t], ref[half + t - 1],
                big_send.at[half + t, which], big_recv.at[half + t, which], mx, sib,
            )
            copy.start()
            forwards.append(copy)

    keyed = []
    returns = []

    def work(src, number):
        rows, inner, count = slots(src)
        own = number == 0
        q_from = q_ref if own else q_in[number - 1]
        g_from = g_ref if own else g_in[number - 1]
        for c in range(cap):
            at = number * cap + c
            r, i = rows[c], inner[c]
            q, g = q_from[r], g_from[r]
            st = st_own[r] if own else st_all[src, r]
            dqt, dk, dv = item(q, g, st, k_ref[i], v_ref[i], kmt[i])
            dk_part[at] = dk
            dv_part[at] = dv
            keyed.append(jnp.where(count > c, i, -1))
            if own:
                ret_in[my * cap + c] = dqt.astype(BF16)
            else:
                ret_out[at] = dqt.astype(BF16)
                copy = remote(
                    ret_out.at[at], ret_in.at[my * cap + c],
                    ret_send.at[at], ret_recv.at[at], mx, src,
                )
                copy.start()
                returns.append(copy)

    work(my, 0)
    pass_on(0)
    wait_big(1, 0)
    wait_big(1, 1)
    for copy in stats:
        copy.wait_recv()
    work(sib, 1)
    pass_on(1)

    for copy in cols:
        copy.wait_recv()
    total = col_all[0]
    for d in range(1, n):
        total = total + col_all[d]
    row_sum[...] = total
    row_all[mx] = total

    def row_copy(t):
        return remote(row_sum, row_all.at[mx], row_send.at[t], row_recv.at[t], xpeer(t), my)

    def send_row(t, carry):
        row_copy(t).start()
        return carry

    lax.fori_loop(1, nx, send_row, 0)

    for t in range(1, half):
        work(lax.rem(my + n - 2 * t, n), 1 + t)
    for t in range(1, half):
        wait_big(half + t, 0)
        wait_big(half + t, 1)
        work(lax.rem(sib + n - 2 * t, n), half + t)

    for b in range(rb):
        dk = dk_acc[b]
        dv = dv_acc[b]
        for at in range(n * cap):
            hit = jnp.full((BLOCK, f), keyed[at], jnp.int32) == b
            dk = dk + jnp.where(hit, dk_part[at], 0.0)
            dv = dv + jnp.where(hit, dv_part[at], 0.0)
        dk_ref[b * BLOCK:(b + 1) * BLOCK] = dk.astype(BF16)
        dv_ref[b * BLOCK:(b + 1) * BLOCK] = dv.astype(BF16)

    def get_row(t, carry):
        row_copy(t).wait_recv()
        return carry

    lax.fori_loop(1, nx, get_row, 0)
    total = lax.fori_loop(1, nx, lambda d, acc: acc + row_all[d], row_all[0])
    sg_ref[...] = total / math.sqrt(pts * nx * n)

    for copy in returns:
        copy.wait_recv()
    place = []
    for r in range(rb):
        for j in range(listed):
            value = nb_s[my, j, r]
            place.append(lax.div(value, rb))
    for r in range(rb):
        dqt = dq_acc[r]
        for j in range(listed):
            e = r * listed + j
            rank = jnp.int32(0)
            for before in range(e):
                rank = rank + (place[before] == place[e]).astype(jnp.int32)
            dqt = dqt + ret_in[place[e] * cap + rank].astype(F32)
        dq_ref[r * BLOCK:(r + 1) * BLOCK] = dqt.T.astype(BF16)

    for copy in halo + lists + stats + big + cols + forwards + returns:
        copy.wait_send()

    def end_row(t, carry):
        row_copy(t).wait_send()
        return carry

    lax.fori_loop(1, nx, end_row, 0)


def write(dq, dk, dv, sg, dq_hbm, dk_hbm, dv_hbm, sg_hbm, sems):
    copies = [
        pltpu.make_async_copy(src, dst, sems.at[at])
        for at, (src, dst) in enumerate(
            [(dq, dq_hbm), (dk, dk_hbm), (dv, dv_hbm), (sg, sg_hbm)]
        )
    ]
    for copy in copies:
        copy.start()
    for copy in copies:
        copy.wait()


def per_device(nx, n, queries, keys, values, out_attn, out_grad, log_norm, neighbour_blocks, stencil):
    tx, ty, f = queries.shape
    pts = tx * ty
    rb = pts // BLOCK
    listed = neighbour_blocks.shape[2]
    cap = max(2, (rb * listed + n - 1) // n)
    flat = [a.reshape(rb, BLOCK, f) for a in (queries, keys, values, out_attn, out_grad)]
    hbm = pl.BlockSpec(memory_space=pltpu.HBM)
    vmem = pl.BlockSpec(memory_space=pltpu.VMEM)
    block_buf = pltpu.VMEM((rb, BLOCK, f), BF16)
    half = n // 2
    dma = pltpu.SemaphoreType.DMA
    grads = jax.ShapeDtypeStruct((pts, f), BF16)
    dq, dk, dv, sg = pl.pallas_call(
        functools.partial(kernel, nx, n, tx, ty, rb, listed, cap),
        out_shape=[pltpu.VMEM((pts, f), BF16)] * 3 + [pltpu.VMEM((8, f), F32)],
        in_specs=[hbm] * 8,
        out_specs=[vmem] * 4,
        scratch_shapes=[
            block_buf, block_buf, block_buf, block_buf, block_buf,
            pltpu.VMEM(log_norm.shape, BF16),
            pltpu.VMEM(stencil.shape, F32),
            pltpu.VMEM((listed, 1, rb), jnp.int32),
            dma((8,)),
            [pltpu.VMEM((rb, BLOCK, f), BF16)] * (n - 1),
            [pltpu.VMEM((rb, BLOCK, f), BF16)] * (n - 1),
            pltpu.VMEM((rb, 2 * HEADS, BLOCK), F32),
            pltpu.VMEM((n, rb, 2 * HEADS, BLOCK), F32),
            pltpu.VMEM((n, 8, 128), jnp.int32),
            pltpu.VMEM((8, 128), jnp.int32),
            pltpu.SMEM((n, 8, 128), jnp.int32),
            pltpu.VMEM((rb, f, HEADS * BLOCK), BF16),
            pltpu.VMEM((2, tx, f), BF16),
            pltpu.VMEM((2, ty, f), BF16),
            pltpu.VMEM((2, tx, f), BF16),
            pltpu.VMEM((rb, f, BLOCK), F32),
            pltpu.VMEM((rb, BLOCK, f), F32),
            pltpu.VMEM((rb, BLOCK, f), F32),
            pltpu.VMEM((n * cap, BLOCK, f), F32),
            pltpu.VMEM((n * cap, BLOCK, f), F32),
            pltpu.VMEM((n * cap, f, BLOCK), BF16),
            pltpu.VMEM((n * cap, f, BLOCK), BF16),
            pltpu.VMEM((8, f), F32),
            pltpu.VMEM((n, 8, f), F32),
            pltpu.VMEM((8, f), F32),
            pltpu.VMEM((nx, 8, f), F32),
            dma((n, 2)), dma((n, 2)),
            dma((n, 2)), dma((n, 2)),
            dma((4,)), dma((4,)),
            dma((n * cap,)), dma((n * cap,)),
            dma((n,)), dma((n,)),
            dma((nx,)), dma((nx,)),
            dma,
        ],
        compiler_params=pltpu.CompilerParams(
            collective_id=0, has_side_effects=True, vmem_limit_bytes=56 * 1024 * 1024
        ),
    )(*flat, log_norm, stencil, neighbour_blocks.transpose(2, 0, 1))
    dq, dk, dv, sg = pl.pallas_call(
        write,
        out_shape=[grads, grads, grads, jax.ShapeDtypeStruct((8, f), F32)],
        in_specs=[vmem] * 4,
        out_specs=[hbm] * 4,
        scratch_shapes=[dma((4,))],
        compiler_params=pltpu.CompilerParams(vmem_limit_bytes=4 * 1024 * 1024),
    )(dq, dk, dv, sg)
    shape = (tx, ty, f)
    return dq.reshape(shape), dk.reshape(shape), dv.reshape(shape), sg[:5]


def solution(mesh):
    placed = (
        P("gx", "gy", None),
        P("gx", "gy", None),
        P("gx", "gy", None),
        P("gx", "gy", None),
        P("gx", "gy", None),
        P(None, "gx", "gy"),
        P("gx", "gy", None),
        P(),
    )
    return jax.shard_map(
        functools.partial(per_device, mesh.shape["gx"], mesh.shape["gy"]),
        mesh=mesh,
        in_specs=placed,
        out_specs=(P("gx", "gy", None), P("gx", "gy", None), P("gx", "gy", None), P()),
        check_vma=False,
    )
```
